768 devices in a mesh: dom: 24 (over z, core), grp: 32 (over x, y).
Axes of the slice: x: 4, y: 8, z: 12, core: 2. Of those that a mesh axis runs over, the one named last changes fastest.
Arguments:
- features: bfloat16 [786432, 256], P(('dom', 'grp')), may hold values from -6 to 6
- w_self: bfloat16 [256, 256], replicated, may hold values from -0.375 to 0.375
- w_neigh: bfloat16 [256, 256], replicated, may hold values from -0.375 to 0.375
- degree: float32 [786432], P(('dom', 'grp')), may hold values from 1 to 8
- send_rows: int32 [18432, 16], P(('dom', 'grp')), may hold values from 0 to 1023, as said below
- inner_tiles: bfloat16 [19968, 128, 128], P(('dom', 'grp')), may hold values from 0.0019989014 to 0.059814453
- inner_blocks: int32 [19968, 2], P(('dom', 'grp')), may hold values from 0 to 10, as said below
- outer_tiles: bfloat16 [11520, 128, 128], P(('dom', 'grp')), may hold values from 0.0019989014 to 0.059814453
- outer_blocks: int32 [11520, 2], P(('dom', 'grp')), may hold values from 0 to 10, as said below
- tile_counts: int32 [768, 2], P(('dom', 'grp')), may hold values from 1 to 26, as said below
- d_out: bfloat16 [786432, 256], P(('dom', 'grp')), may hold values from -6 to 6
- d_mirror: bfloat16 [294912, 256], P(('dom', 'grp')), may hold values from -6 to 6
Outputs:
- out: bfloat16 [786432, 256], P(('dom', 'grp'))
- mirror_out: bfloat16 [294912, 256], P(('dom', 'grp'))
- grad_h: bfloat16 [786432, 256], P(('dom', 'grp'))
- grad_wself: float32 [256, 256], replicated
- grad_wneigh: float32 [256, 256], replicated
The draws below stay inside these ranges and needn't reach their ends.
Inputs may be any that keep to these rules, and one draw needn't show every extreme that they name: `send_rows`: the 16 rows that one device lists for one peer are distinct. `inner_blocks`: each row is (destination block, source block) of slot blocks of 128 rows; the pairs of one device are distinct; sources are master blocks. `outer_blocks`: each row is (destination block, source block); the pairs of one device are distinct; sources are mirror blocks, from 8 on; destinations any block. `tile_counts`: column 0 counts the live leading inner tiles of a device, at most 26; column 1 the live outer tiles, at most 15; in every draw some device has 26 live inner tiles and some device 15 live outer tiles.
All inputs are finite; a program needn't handle non-finite values.
Results may differ from the reference program's by a relative error of at most 0.0057.
Values may be sent and summed in bfloat16 or wider, within the bound.
No kernel may reach another device: no remote copies, remote signals or barrier semaphores. Data moves between devices by JAX's collectives and lax.ppermute only.
A program may use at most 64 MiB of HBM per device.

```python
import math
import jax
import jax.numpy as jnp
from jax import lax

D = 256
BLOCK = 128
V = 1024
MIRRORS = 384
S = 16
K_IN = 26
K_OUT = 15
VERTICES = 786432
N_DOM = 24
N_GRP = 32
DEVICES = 768


def tile_pairs(key, capacity, source_low, source_blocks):
    total_blocks = (V + MIRRORS) // BLOCK
    keys = jax.random.split(key, DEVICES)
    chosen = jax.vmap(lambda one_key: jax.random.permutation(one_key, total_blocks * source_blocks)[:capacity])(keys)
    target = chosen // source_blocks
    source = source_low + chosen % source_blocks
    return jnp.stack([target, source], axis=-1).reshape(DEVICES * capacity, 2).astype(jnp.int32)


def draw_send_rows(key, part):
    key = jax.random.fold_in(key, 1)
    keys = jax.random.split(key, DEVICES * N_DOM)
    chosen = jax.vmap(lambda one_key: jax.random.permutation(one_key, V)[:S])(keys)
    return chosen.astype(jnp.int32)


def draw_inner_blocks(key, part):
    key = jax.random.fold_in(key, 2)
    return tile_pairs(key, K_IN, 0, V // BLOCK)


def draw_outer_blocks(key, part):
    key = jax.random.fold_in(key, 3)
    return tile_pairs(key, K_OUT, V // BLOCK, MIRRORS // BLOCK)


def busy_counts(key, capacity):
    first, second = jax.random.split(key)
    counts = jax.random.randint(first, (DEVICES,), max(1, capacity // 4), capacity + 1)
    busiest = jax.random.randint(second, (), 0, DEVICES)
    return counts.at[busiest].set(capacity)


def draw_tile_counts(key, part):
    key = jax.random.fold_in(key, 4)
    first, second = jax.random.split(key)
    return jnp.stack([busy_counts(first, K_IN), busy_counts(second, K_OUT)], axis=-1).astype(jnp.int32)


def shard_levels(stream_key, dims, cuts, least, largest):
    factor_of = 1.0
    for position, blocks in cuts:
        draws = jax.random.uniform(jax.random.fold_in(jax.random.fold_in(stream_key, 6), position), (blocks,), jnp.float32, least / len(cuts), largest / len(cuts))
        factor_of = factor_of * jnp.repeat(jnp.exp(draws), dims[position] // blocks).reshape((-1,) + (1,) * (len(dims) - 1 - position))
    return factor_of


def noise(key, dims, width, limit, cuts=(), kind=jnp.bfloat16):
    drawn = jax.random.normal(key, dims, jnp.float32) * width
    if len(cuts) > 0:
        drawn = shard_levels(key, dims, cuts, -0.22, 0.18) * drawn
    return jnp.clip(drawn, min=-limit, max=limit).astype(kind)


def setup_inputs(seed: int = 0) -> dict:
    arg_keys = jax.random.split(jax.random.key(seed), 13)
    features = noise(arg_keys[0], (VERTICES, D), 1.0, 6.0, ((0, 768),))
    w_self = noise(arg_keys[1], (D, D), D ** -0.5, 0.375)
    w_neigh = noise(arg_keys[2], (D, D), D ** -0.5, 0.375)
    degree = jnp.clip(jnp.exp(math.log(8.0) - 2.0794415 * jax.random.uniform(arg_keys[3], (VERTICES,), jnp.float32) ** shard_levels(arg_keys[3], (VERTICES,), ((0, 768),), -0.2, 0.2)), 1.0, 8.0)
    send_rows = draw_send_rows(jax.random.fold_in(arg_keys[12], 71), 0)
    inner_tiles = jnp.clip(jnp.exp(math.log(0.059814453) - 3.3986496 * jax.random.uniform(arg_keys[5], (DEVICES * K_IN, BLOCK, BLOCK), jnp.float32) ** shard_levels(arg_keys[5], (DEVICES * K_IN, BLOCK, BLOCK), ((0, 768),), -0.2, 0.2)), 0.0019989014, 0.059814453).astype(jnp.bfloat16)
    inner_blocks = draw_inner_blocks(jax.random.fold_in(arg_keys[12], 71), 0)
    outer_tiles = jnp.clip(jnp.exp(math.log(0.059814453) - 3.3986496 * jax.random.uniform(arg_keys[7], (DEVICES * K_OUT, BLOCK, BLOCK), jnp.float32) ** shard_levels(arg_keys[7], (DEVICES * K_OUT, BLOCK, BLOCK), ((0, 768),), -0.2, 0.2)), 0.0019989014, 0.059814453).astype(jnp.bfloat16)
    outer_blocks = draw_outer_blocks(jax.random.fold_in(arg_keys[12], 71), 0)
    tile_counts = draw_tile_counts(jax.random.fold_in(arg_keys[12], 71), 0)
    d_out = noise(arg_keys[10], (VERTICES, D), 1.0, 6.0, ((0, 768),))
    d_mirror = noise(arg_keys[11], (DEVICES * MIRRORS, D), 1.0, 6.0, ((0, 768),))
    return dict(features=features, w_self=w_self, w_neigh=w_neigh, degree=degree, send_rows=send_rows, inner_tiles=inner_tiles, inner_blocks=inner_blocks, outer_tiles=outer_tiles, outer_blocks=outer_blocks, tile_counts=tile_counts, d_out=d_out, d_mirror=d_mirror)


def tile_sum(slot_rows, tile_list, blocks, count):
    total_blocks = slot_rows.shape[0] // BLOCK
    grouped = slot_rows.reshape(total_blocks, BLOCK, -1)
    sources = grouped[blocks[:, 1]].astype(jnp.float32)
    alive = (jnp.arange(tile_list.shape[0]) < count).astype(jnp.float32)
    product = jnp.einsum('kij,kjd->kid', tile_list.astype(jnp.float32), sources) * alive[:, None, None]
    result = jnp.zeros(grouped.shape, jnp.float32).at[blocks[:, 0]].add(product)
    return result.reshape(slot_rows.shape[0], -1)

def tile_back(slot_rows, tile_list, blocks, count):
    total_blocks = slot_rows.shape[0] // BLOCK
    grouped = slot_rows.reshape(total_blocks, BLOCK, -1)
    targets = grouped[blocks[:, 0]].astype(jnp.float32)
    alive = (jnp.arange(tile_list.shape[0]) < count).astype(jnp.float32)
    product = jnp.einsum('kij,kid->kjd', tile_list.astype(jnp.float32), targets) * alive[:, None, None]
    result = jnp.zeros(grouped.shape, jnp.float32).at[blocks[:, 1]].add(product)
    return result.reshape(slot_rows.shape[0], -1)

def finish(z_value):
    silu_value = jax.nn.silu(z_value)
    return silu_value * lax.rsqrt(lax.optimization_barrier(jnp.mean(silu_value * silu_value, axis=-1, keepdims=True)) + 1e-05)

def reference(features, w_self, w_neigh, degree, send_rows, inner_tiles, inner_blocks, outer_tiles, outer_blocks, tile_counts, d_out, d_mirror):
    lists = send_rows.reshape(N_DOM, N_GRP, N_DOM, S)

    def spread(master_vals):
        picked = jax.vmap(jax.vmap(lambda values, index: values[index]))(master_vals, lists)
        return picked.transpose(2, 1, 0, 3, 4).reshape(N_DOM, N_GRP, MIRRORS, D)

    def collect(mirror_vals):
        returned = mirror_vals.reshape(N_DOM, N_GRP, N_DOM, S, D).transpose(2, 1, 0, 3, 4)

        def one_device(pieces, index):
            return jnp.zeros((V, D), jnp.float32).at[index.reshape(-1)].add(pieces.reshape(-1, D).astype(jnp.float32))
        return jax.vmap(jax.vmap(one_device))(returned, lists)
    inner_t = inner_tiles.reshape(DEVICES, K_IN, BLOCK, BLOCK)
    inner_b = inner_blocks.reshape(DEVICES, K_IN, 2)
    outer_t = outer_tiles.reshape(DEVICES, K_OUT, BLOCK, BLOCK)
    outer_b = outer_blocks.reshape(DEVICES, K_OUT, 2)
    counts = tile_counts.reshape(DEVICES, 2)

    def apply_tiles(step_fn, slot_all):

        def one_device(entry):
            return step_fn(entry[0], entry[1], entry[2], entry[5][0]) + step_fn(entry[0], entry[3], entry[4], entry[5][1])
        return lax.map(one_device, (slot_all, inner_t, inner_b, outer_t, outer_b, counts)).reshape(N_DOM, N_GRP, V + MIRRORS, D)
    master_h = features.reshape(N_DOM, N_GRP, V, D)
    slot_h = jnp.concatenate([master_h, spread(master_h)], axis=2).reshape(DEVICES, V + MIRRORS, D)
    partial_value = apply_tiles(tile_sum, slot_h)
    mirror_part = partial_value[:, :, V:].astype(jnp.bfloat16)
    aggregate = partial_value[:, :, :V] + collect(mirror_part)
    degree_col = degree.reshape(-1, 1)
    average = (aggregate.reshape(-1, D) / degree_col).astype(jnp.bfloat16)
    z_value = jnp.dot(features, w_self, preferred_element_type=jnp.float32) + jnp.dot(average, w_neigh, preferred_element_type=jnp.float32)
    out_full, pullback = jax.vjp(finish, z_value)
    out = out_full.astype(jnp.bfloat16)
    mirror_out = spread(out.reshape(N_DOM, N_GRP, V, D)).reshape(-1, D)
    g_out = d_out.astype(jnp.float32) + collect(d_mirror.reshape(N_DOM, N_GRP, MIRRORS, D)).reshape(-1, D)
    dz_value = pullback(g_out)[0].astype(jnp.bfloat16)
    grad_wself = jnp.dot(features.T, dz_value, preferred_element_type=jnp.float32)
    grad_wneigh = jnp.dot(average.T, dz_value, preferred_element_type=jnp.float32)
    d_avg = (jnp.dot(dz_value, w_neigh.T, preferred_element_type=jnp.float32) / degree_col).astype(jnp.bfloat16)
    self_part = jnp.dot(dz_value, w_self.T, preferred_element_type=jnp.float32)
    avg_master = d_avg.reshape(N_DOM, N_GRP, V, D)
    slot_g = jnp.concatenate([avg_master, spread(avg_master)], axis=2).reshape(DEVICES, V + MIRRORS, D)
    back = apply_tiles(tile_back, slot_g)
    mirror_back = back[:, :, V:].astype(jnp.bfloat16)
    grad_full = self_part.reshape(N_DOM, N_GRP, V, D) + back[:, :, :V] + collect(mirror_back)
    grad_h = grad_full.reshape(-1, D).astype(jnp.bfloat16)
    return (out, mirror_out, grad_h, grad_wself, grad_wneigh)
```

```python
import functools

import jax
import jax.numpy as jnp
from jax import lax
from jax.experimental import pallas as pl
from jax.experimental.pallas import tpu as pltpu
from jax.sharding import Mesh, PartitionSpec as P

BLOCK = 128
BF16 = jnp.bfloat16
F32 = jnp.float32
NN = (((1,), (0,)), ((), ()))
TN = (((0,), (0,)), ((), ()))
NT = (((1,), (1,)), ((), ()))


def dot(a, b, dims=NN):
    return lax.dot_general(a, b, dims, preferred_element_type=F32)


def index_column(send):
    peers, each = send.shape
    total = peers * each
    pick = lax.broadcasted_iota(jnp.int32, (total, peers), 0) // each == lax.broadcasted_iota(
        jnp.int32, (total, peers), 1
    )
    pick = jnp.where(pick, 1.0, 0.0).astype(BF16)
    high = dot(pick, (send >> 5).astype(F32).astype(BF16))
    low = dot(pick, (send & 31).astype(F32).astype(BF16))
    full = high * 32.0 + low
    lane = lax.broadcasted_iota(jnp.int32, (total, each), 1)
    row = lax.broadcasted_iota(jnp.int32, (total, each), 0)
    mine = jnp.where(lane == row % each, full, 0.0)
    return jnp.sum(mine, axis=1, keepdims=True).astype(jnp.int32)


def gather_matrix(send, rows):
    column = index_column(send)
    place = lax.broadcasted_iota(jnp.int32, (column.shape[0], rows), 1)
    return jnp.where(place == column, 1.0, 0.0).astype(BF16)


def scatter_matrix(flat, rows):
    place = lax.broadcasted_iota(jnp.int32, (rows, flat.shape[1]), 0)
    return jnp.where(place == flat, 1.0, 0.0).astype(BF16)


def gather_kernel(send_ref, x_ref, o_ref):
    o_ref[...] = dot(gather_matrix(send_ref[...], x_ref.shape[0]), x_ref[...]).astype(BF16)


def adjacency_kernel(
    counts_ref, ib_ref, ob_ref, it_ref, ot_ref, x_ref, master_ref, mirror_ref, part_ref
):
    masters = x_ref.shape[0] // BLOCK
    blocks = master_ref.shape[0] // BLOCK
    mirrors = blocks - masters
    master_ref[...] = jnp.zeros_like(master_ref)
    mirror_ref[...] = jnp.zeros_like(mirror_ref)

    def place(tiles, table, count, into, first):
        def step(k, carry):
            @pl.when(k < count)
            def _():
                dst = table[k, 0]
                dst = jnp.where(dst >= masters, dst - masters, dst + mirrors)
                src = table[k, 1] - first
                rows = pl.ds(pl.multiple_of(dst * BLOCK, BLOCK), BLOCK)
                cols = pl.ds(pl.multiple_of(src * BLOCK, BLOCK), BLOCK)
                into[rows, cols] = tiles[k]

            return carry

        lax.fori_loop(0, tiles.shape[0], step, 0)

    place(it_ref, ib_ref, counts_ref[0, 0], master_ref, 0)
    place(ot_ref, ob_ref, counts_ref[0, 1], mirror_ref, masters)
    part_ref[...] = dot(master_ref[...], x_ref[...])


def mirror_part_kernel(part_ref, a_ref, h_ref, o_ref):
    o_ref[...] = (part_ref[...] + dot(a_ref[...], h_ref[...])).astype(BF16)


def master_part_kernel(part_ref, a_ref, h_ref, x_ref, w_ref, flat_ref, d_ref, r_ref, p_ref, z_ref, g_ref):
    m = h_ref.shape[0]
    p_ref[...] = part_ref[m:, :] + dot(a_ref[m:, :], h_ref[...])
    z_ref[...] = dot(x_ref[...], w_ref[...])
    g_ref[...] = d_ref[...].astype(F32) + dot(scatter_matrix(flat_ref[...], x_ref.shape[0]), r_ref[...])


def dense_kernel(
    send_ref, flat_ref, deg_ref, p_ref, z_ref, g_ref, r_ref, w_ref,
    avg_ref, out_ref, dz_ref, davg_ref, pick_ref,
):
    rows, width = p_ref.shape
    total = p_ref[...] + dot(scatter_matrix(flat_ref[...], rows), r_ref[...])
    degree = deg_ref[...]
    avg = (total / degree).astype(BF16)
    avg_ref[...] = avg
    z = z_ref[...] + dot(avg, w_ref[...])
    s = jax.nn.sigmoid(z)
    u = z * s
    scale = lax.rsqrt(jnp.mean(u * u, axis=1, keepdims=True) + 1e-05)
    n = u * scale
    out_ref[...] = n.astype(BF16)
    g = g_ref[...]
    du = scale * (g - n * jnp.mean(g * n, axis=1, keepdims=True))
    dz = (du * (s * (1.0 + z * (1.0 - s)))).astype(BF16)
    dz_ref[...] = dz
    davg = (dot(dz, w_ref[...], NT) / degree).astype(BF16)
    davg_ref[...] = davg
    pick_ref[...] = dot(gather_matrix(send_ref[...], rows), davg).astype(BF16)


def weight_kernel(x_ref, avg_ref, dz_ref, o_ref):
    d = x_ref.shape[1]
    o_ref[:d, :] = dot(x_ref[...], dz_ref[...], TN)
    o_ref[d:, :] = dot(avg_ref[...], dz_ref[...], TN)


def back_kernel(dz_ref, w_ref, davg_ref, am_ref, ar_ref, o_ref, r_ref):
    m = ar_ref.shape[1]
    o_ref[...] = dot(dz_ref[...], w_ref[...], NT) + dot(am_ref[m:, :], davg_ref[...], TN)
    r_ref[...] = dot(ar_ref[m:, :], davg_ref[...], TN)


def mirror_back_kernel(back_ref, a_ref, g_ref, o_ref):
    o_ref[...] = (back_ref[...] + dot(a_ref[...], g_ref[...], TN)).astype(BF16)


def master_back_kernel(back_ref, a_ref, g_ref, o_ref):
    o_ref[...] = back_ref[...] + dot(a_ref[...], g_ref[...], TN)


def grad_kernel(flat_ref, back_ref, r_ref, o_ref):
    rows = back_ref.shape[0]
    o_ref[...] = (back_ref[...] + dot(scatter_matrix(flat_ref[...], rows), r_ref[...])).astype(BF16)


def reduce_terms(terms, dom, grp):
    return lax.psum(lax.psum(terms, dom), grp)


VMEM = pl.BlockSpec(memory_space=pltpu.VMEM)
SMEM = pl.BlockSpec(memory_space=pltpu.SMEM)
ROOM = 40 * 1024 * 1024


def sds(shape, dtype):
    return jax.ShapeDtypeStruct(shape, dtype)


def call(body, out, args, specs=None, flops=0, name=None):
    many = isinstance(out, tuple)
    moved = sum(a.size * a.dtype.itemsize for a in args) + sum(
        o.size * o.dtype.itemsize for o in (out if many else (out,))
    )
    return pl.pallas_call(
        body,
        grid=(1,),
        out_shape=out,
        in_specs=specs or [VMEM] * len(args),
        out_specs=tuple([VMEM] * len(out)) if many else VMEM,
        compiler_params=pltpu.CompilerParams(vmem_limit_bytes=ROOM),
        cost_estimate=pl.CostEstimate(flops=flops, bytes_accessed=moved, transcendentals=0),
        name=name,
    )(*args)


def head(rows, cols):
    return pl.BlockSpec((rows, cols), lambda i: (0, 0))


def on_device(
    dom,
    grp,
    features,
    w_self,
    w_neigh,
    degree,
    send_rows,
    inner_tiles,
    inner_blocks,
    outer_tiles,
    outer_blocks,
    tile_counts,
    d_out,
    d_mirror,
):
    rows, width = features.shape
    peers, each = send_rows.shape
    mirrors = peers * each
    slots = rows + mirrors
    mm = 2 * width

    def exchange(values):
        return lax.all_to_all(
            values.reshape(peers, each, width), dom, split_axis=0, concat_axis=0, tiled=True
        ).reshape(mirrors, width)

    def gather(values, name):
        return call(
            gather_kernel, sds((mirrors, width), BF16), (send_rows, values),
            flops=mm * mirrors * rows, name=name,
        )

    flat = send_rows.reshape(1, mirrors)
    degree_col = degree[:, None]

    mirror_h = exchange(gather(features, "pick_h"))
    d_back = exchange(d_mirror)
    a_master, a_mirror, part = call(
        adjacency_kernel,
        (sds((slots, rows), BF16), sds((slots, mirrors), BF16), sds((slots, width), F32)),
        (tile_counts, inner_blocks, outer_blocks, inner_tiles, outer_tiles, features),
        specs=[SMEM] * 3 + [VMEM] * 3,
        flops=mm * slots * rows,
        name="adjacency",
    )
    mirror_part = call(
        mirror_part_kernel, sds((mirrors, width), BF16), (part, a_mirror, mirror_h),
        specs=[head(mirrors, width), head(mirrors, mirrors), VMEM],
        flops=mm * mirrors * mirrors, name="mirror_part",
    )
    got_part = exchange(mirror_part)
    p_master, z_self, g_out = call(
        master_part_kernel, (sds((rows, width), F32),) * 3,
        (part, a_mirror, mirror_h, features, w_self, flat, d_out, d_back),
        flops=mm * rows * (2 * mirrors + width), name="master_part",
    )
    avg, out, dz, d_avg, pick_g = call(
        dense_kernel, (sds((rows, width), BF16),) * 4 + (sds((mirrors, width), BF16),),
        (send_rows, flat, degree_col, p_master, z_self, g_out, got_part, w_neigh),
        flops=mm * rows * (2 * mirrors + 2 * width), name="dense",
    )
    mirror_g = exchange(pick_g)
    terms = call(
        weight_kernel, sds((2 * width, width), F32), (features, avg, dz),
        flops=2 * mm * rows * width, name="weights",
    )
    sums = reduce_terms(terms, dom, grp)
    mirror_out = exchange(gather(out, "pick_out"))
    back, back_mirror = call(
        back_kernel, (sds((rows, width), F32), sds((mirrors, width), F32)),
        (dz, w_self, d_avg, a_master, a_mirror),
        flops=mm * rows * (width + slots), name="back",
    )
    mirror_back = call(
        mirror_back_kernel, sds((mirrors, width), BF16), (back_mirror, a_mirror, mirror_g),
        specs=[VMEM, head(mirrors, mirrors), VMEM],
        flops=mm * mirrors * mirrors, name="mirror_back",
    )
    got_back = exchange(mirror_back)
    back = call(
        master_back_kernel, sds((rows, width), F32), (back, a_master, mirror_g),
        specs=[VMEM, head(mirrors, rows), VMEM],
        flops=mm * rows * mirrors, name="master_back",
    )
    grad_h = call(
        grad_kernel, sds((rows, width), BF16), (flat, back, got_back),
        flops=mm * rows * mirrors, name="grad",
    )
    return (out, mirror_out, grad_h, sums[:width], sums[width:])


def solution(mesh):
    names = ("dom", "grp")
    split = lambda rank: P(names, *([None] * (rank - 1)))
    in_specs = (
        split(2), P(), P(), split(1), split(2), split(3), split(2), split(3), split(2), split(2),
        split(2), split(2),
    )
    out_specs = (split(2), split(2), split(2), P(), P())
    return jax.shard_map(
        functools.partial(on_device, "dom", "grp"),
        mesh=mesh, in_specs=in_specs, out_specs=out_specs, check_vma=False,
    )
```

```python
import functools

import jax
import jax.numpy as jnp
from jax import lax
from jax.experimental import pallas as pl
from jax.experimental.pallas import tpu as pltpu
from jax.sharding import Mesh, PartitionSpec as P

BLOCK = 128
BF16 = jnp.bfloat16
F32 = jnp.float32
NN = (((1,), (0,)), ((), ()))
TN = (((0,), (0,)), ((), ()))
NT = (((1,), (1,)), ((), ()))


def dot(a, b, dims=NN):
    return lax.dot_general(a, b, dims, preferred_element_type=F32)


def index_column(send):
    peers, each = send.shape
    total = peers * each
    pick = lax.broadcasted_iota(jnp.int32, (total, peers), 0) // each == lax.broadcasted_iota(
        jnp.int32, (total, peers), 1
    )
    pick = jnp.where(pick, 1.0, 0.0).astype(BF16)
    high = dot(pick, (send >> 5).astype(F32).astype(BF16))
    low = dot(pick, (send & 31).astype(F32).astype(BF16))
    full = high * 32.0 + low
    lane = lax.broadcasted_iota(jnp.int32, (total, each), 1)
    row = lax.broadcasted_iota(jnp.int32, (total, each), 0)
    mine = jnp.where(lane == row % each, full, 0.0)
    return jnp.sum(mine, axis=1, keepdims=True).astype(jnp.int32)


def gather_matrix(send, rows):
    column = index_column(send)
    place = lax.broadcasted_iota(jnp.int32, (column.shape[0], rows), 1)
    return jnp.where(place == column, 1.0, 0.0).astype(BF16)


def scatter_matrix(flat, rows):
    place = lax.broadcasted_iota(jnp.int32, (rows, flat.shape[1]), 0)
    return jnp.where(place == flat, 1.0, 0.0).astype(BF16)


def put_pieces(o_ref, first, rows):
    each = o_ref.shape[1] // 2
    o_ref[:, first * each : (first + 1) * each, :] = rows.reshape(o_ref.shape[0], each, o_ref.shape[2])


def get_pieces(ref, which):
    each = ref.shape[1] // 2
    return ref[:, which * each : (which + 1) * each, :].reshape(ref.shape[0] * each, ref.shape[2])


def first_kernel(send_ref, x_ref, d_ref, o_ref):
    put_pieces(o_ref, 0, dot(gather_matrix(send_ref[...], x_ref.shape[0]), x_ref[...]).astype(BF16))
    put_pieces(o_ref, 1, d_ref[...])


def adjacency_kernel(
    counts_ref, ib_ref, ob_ref, it_ref, ot_ref, x_ref, master_ref, mirror_ref, part_ref
):
    masters = x_ref.shape[0] // BLOCK
    blocks = master_ref.shape[0] // BLOCK
    mirrors = blocks - masters
    master_ref[...] = jnp.zeros_like(master_ref)
    mirror_ref[...] = jnp.zeros_like(mirror_ref)

    def place(tiles, table, count, into, first):
        def step(k, carry):
            @pl.when(k < count)
            def _():
                dst = table[k, 0]
                dst = jnp.where(dst >= masters, dst - masters, dst + mirrors)
                src = table[k, 1] - first
                rows = pl.ds(pl.multiple_of(dst * BLOCK, BLOCK), BLOCK)
                cols = pl.ds(pl.multiple_of(src * BLOCK, BLOCK), BLOCK)
                into[rows, cols] = tiles[k]

            return carry

        lax.fori_loop(0, tiles.shape[0], step, 0)

    place(it_ref, ib_ref, counts_ref[0, 0], master_ref, 0)
    place(ot_ref, ob_ref, counts_ref[0, 1], mirror_ref, masters)
    part_ref[...] = dot(master_ref[...], x_ref[...])


def mirror_part_kernel(part_ref, a_ref, got_ref, o_ref):
    o_ref[...] = (part_ref[...] + dot(a_ref[...], get_pieces(got_ref, 0))).astype(BF16)


def master_part_kernel(part_ref, a_ref, got_ref, x_ref, w_ref, flat_ref, d_ref, p_ref, z_ref, g_ref):
    m = a_ref.shape[1]
    p_ref[...] = part_ref[m:, :] + dot(a_ref[m:, :], get_pieces(got_ref, 0))
    z_ref[...] = dot(x_ref[...], w_ref[...])
    spread = scatter_matrix(flat_ref[...], x_ref.shape[0])
    g_ref[...] = d_ref[...].astype(F32) + dot(spread, get_pieces(got_ref, 1))


def dense_kernel(
    send_ref, flat_ref, deg_ref, p_ref, z_ref, g_ref, r_ref, w_ref,
    avg_ref, out_ref, dz_ref, davg_ref, pick_ref,
):
    rows, width = p_ref.shape
    total = p_ref[...] + dot(scatter_matrix(flat_ref[...], rows), r_ref[...])
    degree = deg_ref[...]
    avg = (total / degree).astype(BF16)
    avg_ref[...] = avg
    z = z_ref[...] + dot(avg, w_ref[...])
    s = jax.nn.sigmoid(z)
    u = z * s
    scale = lax.rsqrt(jnp.mean(u * u, axis=1, keepdims=True) + 1e-05)
    n = u * scale
    out_ref[...] = n.astype(BF16)
    g = g_ref[...]
    du = scale * (g - n * jnp.mean(g * n, axis=1, keepdims=True))
    dz = (du * (s * (1.0 + z * (1.0 - s)))).astype(BF16)
    dz_ref[...] = dz
    davg = (dot(dz, w_ref[...], NT) / degree).astype(BF16)
    davg_ref[...] = davg
    chosen = gather_matrix(send_ref[...], rows)
    put_pieces(pick_ref, 0, dot(chosen, davg).astype(BF16))
    put_pieces(pick_ref, 1, dot(chosen, n.astype(BF16)).astype(BF16))


def weight_kernel(x_ref, avg_ref, dz_ref, o_ref):
    half = o_ref.shape[0] // 2
    piece = (half,) + o_ref.shape[1:]
    o_ref[:half] = dot(x_ref[...], dz_ref[...], TN).astype(BF16).reshape(piece)
    o_ref[half:] = dot(avg_ref[...], dz_ref[...], TN).astype(BF16).reshape(piece)


def back_kernel(dz_ref, w_ref, davg_ref, am_ref, ar_ref, o_ref, r_ref):
    m = ar_ref.shape[1]
    o_ref[...] = dot(dz_ref[...], w_ref[...], NT) + dot(am_ref[m:, :], davg_ref[...], TN)
    r_ref[...] = dot(ar_ref[m:, :], davg_ref[...], TN)


def mirror_back_kernel(back_ref, a_ref, got_ref, terms_ref, o_ref):
    rows = back_ref[...] + dot(a_ref[...], get_pieces(got_ref, 0), TN)
    put_pieces(o_ref, 0, rows.astype(BF16))
    each = terms_ref.shape[1]
    total = jnp.sum(terms_ref[...].astype(F32), axis=0).astype(BF16)
    o_ref[:, each:, :] = jnp.broadcast_to(total[None], (o_ref.shape[0],) + total.shape)


def master_back_kernel(back_ref, a_ref, got_ref, o_ref, out_ref):
    o_ref[...] = back_ref[...] + dot(a_ref[...], get_pieces(got_ref, 0), TN)
    out_ref[...] = get_pieces(got_ref, 1)


def share_kernel(got_ref, o_ref):
    each = o_ref.shape[1]
    total = jnp.sum(got_ref[:, each:, :].astype(F32), axis=0).astype(BF16)
    o_ref[...] = jnp.broadcast_to(total[None], o_ref.shape)


def grad_kernel(flat_ref, back_ref, got_ref, o_ref):
    rows = back_ref.shape[0]
    spread = scatter_matrix(flat_ref[...], rows)
    o_ref[...] = (back_ref[...] + dot(spread, get_pieces(got_ref, 0))).astype(BF16)


def widen_kernel(x_ref, self_ref, neigh_ref):
    half = x_ref.shape[0] // 2
    self_ref[...] = x_ref[:half].reshape(self_ref.shape).astype(F32)
    neigh_ref[...] = x_ref[half:].reshape(neigh_ref.shape).astype(F32)


VMEM = pl.BlockSpec(memory_space=pltpu.VMEM)
SMEM = pl.BlockSpec(memory_space=pltpu.SMEM)
ROOM = 60 * 1024 * 1024


def sds(shape, dtype):
    return jax.ShapeDtypeStruct(shape, dtype)


def call(body, out, args, specs=None, flops=0, name=None):
    many = isinstance(out, tuple)
    moved = sum(a.size * a.dtype.itemsize for a in args) + sum(
        o.size * o.dtype.itemsize for o in (out if many else (out,))
    )
    return pl.pallas_call(
        body,
        grid=(1,),
        out_shape=out,
        in_specs=specs or [VMEM] * len(args),
        out_specs=tuple([VMEM] * len(out)) if many else VMEM,
        compiler_params=pltpu.CompilerParams(vmem_limit_bytes=ROOM),
        cost_estimate=pl.CostEstimate(flops=flops, bytes_accessed=moved, transcendentals=0),
        name=name,
    )(*args)


def head(rows, cols):
    return pl.BlockSpec((rows, cols), lambda i: (0, 0))


def on_device(
    dom,
    grp,
    features,
    w_self,
    w_neigh,
    degree,
    send_rows,
    inner_tiles,
    inner_blocks,
    outer_tiles,
    outer_blocks,
    tile_counts,
    d_out,
    d_mirror,
):
    rows, width = features.shape
    peers, each = send_rows.shape
    mirrors = peers * each
    slots = rows + mirrors
    mm = 2 * width

    groups = lax.axis_size(grp)
    share = 2 * width // groups

    def exchange(values, axis):
        return lax.all_to_all(values, axis, split_axis=0, concat_axis=0, tiled=True)

    single = sds((peers, each, width), BF16)
    double = sds((peers, 2 * each, width), BF16)
    flat = send_rows.reshape(1, mirrors)
    degree_col = degree[:, None]

    pick_h = call(
        first_kernel, double, (send_rows, features, d_mirror),
        flops=mm * mirrors * rows, name="pick_h",
    )
    got_h = exchange(pick_h, dom)
    a_master, a_mirror, part = call(
        adjacency_kernel,
        (sds((slots, rows), BF16), sds((slots, mirrors), BF16), sds((slots, width), F32)),
        (tile_counts, inner_blocks, outer_blocks, inner_tiles, outer_tiles, features),
        specs=[SMEM] * 3 + [VMEM] * 3,
        flops=mm * slots * rows,
        name="adjacency",
    )
    mirror_part = call(
        mirror_part_kernel, sds((mirrors, width), BF16), (part, a_mirror, got_h),
        specs=[head(mirrors, width), head(mirrors, mirrors), VMEM],
        flops=mm * mirrors * mirrors, name="mirror_part",
    )
    got_part = exchange(mirror_part.reshape(single.shape), dom).reshape(mirrors, width)
    p_master, z_self, g_out = call(
        master_part_kernel, (sds((rows, width), F32),) * 3,
        (part, a_mirror, got_h, features, w_self, flat, d_out),
        flops=mm * rows * (2 * mirrors + width), name="master_part",
    )
    avg, out, dz, d_avg, pick_g = call(
        dense_kernel, (sds((rows, width), BF16),) * 4 + (double,),
        (send_rows, flat, degree_col, p_master, z_self, g_out, got_part, w_neigh),
        flops=mm * rows * (2 * mirrors + 2 * width), name="dense",
    )
    got_g = exchange(pick_g, dom)
    terms = call(
        weight_kernel, sds((groups, share, width), BF16), (features, avg, dz),
        flops=2 * mm * rows * width, name="weights",
    )
    got_terms = exchange(terms, grp)
    back, back_mirror = call(
        back_kernel, (sds((rows, width), F32), sds((mirrors, width), F32)),
        (dz, w_self, d_avg, a_master, a_mirror),
        flops=mm * rows * (width + slots), name="back",
    )
    mirror_back = call(
        mirror_back_kernel, double, (back_mirror, a_mirror, got_g, got_terms),
        specs=[VMEM, head(mirrors, mirrors), VMEM, VMEM],
        flops=mm * mirrors * mirrors, name="mirror_back",
    )
    got_back = exchange(mirror_back, dom)
    back, mirror_out = call(
        master_back_kernel, (sds((rows, width), F32), sds((mirrors, width), BF16)),
        (back, a_master, got_g),
        specs=[VMEM, head(mirrors, rows), VMEM],
        flops=mm * rows * mirrors, name="master_back",
    )
    totals = exchange(call(share_kernel, sds((groups, share, width), BF16), (got_back,), name="share"), grp)
    grad_h = call(
        grad_kernel, sds((rows, width), BF16), (flat, back, got_back),
        flops=mm * rows * mirrors, name="grad",
    )
    grad_wself, grad_wneigh = call(
        widen_kernel, (sds((width, width), F32),) * 2, (totals,), name="widen"
    )
    return (out, mirror_out, grad_h, grad_wself, grad_wneigh)


def solution(mesh):
    names = ("dom", "grp")
    split = lambda rank: P(names, *([None] * (rank - 1)))
    in_specs = (
        split(2), P(), P(), split(1), split(2), split(3), split(2), split(3), split(2), split(2),
        split(2), split(2),
    )
    out_specs = (split(2), split(2), split(2), P(), P())
    return jax.shard_map(
        functools.partial(on_device, "dom", "grp"),
        mesh=mesh, in_specs=in_specs, out_specs=out_specs, check_vma=False,
    )
```

```python
import functools

import jax
import jax.numpy as jnp
from jax import lax
from jax.experimental import pallas as pl
from jax.experimental.pallas import tpu as pltpu
from jax.sharding import PartitionSpec as P

BLOCK = 128
HALF = 128
TILE = 16
BF16 = jnp.bfloat16
F32 = jnp.float32
NN = (((1,), (0,)), ((), ()))
TN = (((0,), (0,)), ((), ()))
NT = (((1,), (1,)), ((), ()))
ROOM = 62_500_000


def dot(a, b, dims=NN):
    return lax.dot_general(a, b, dims, preferred_element_type=F32)


def one_hot(mask):
    return jnp.where(mask, 1.0, 0.0).astype(BF16)


def iota(shape, dim):
    return lax.broadcasted_iota(jnp.int32, shape, dim)


def narrow(value):
    return value.astype(F32).astype(BF16)


def index_column(send):
    each, peers = send.shape
    total = each * peers
    pick = one_hot(iota((total, peers), 0) // each == iota((total, peers), 1))
    full = dot(pick, narrow(send >> 5), NT) * 32.0 + dot(pick, narrow(send & 31), NT)
    mine = jnp.where(iota((total, each), 1) == iota((total, each), 0) % each, full, 0.0)
    return jnp.sum(mine, axis=1, keepdims=True).astype(jnp.int32)


def index_row(send):
    each, peers = send.shape
    total = each * peers
    pick = one_hot(iota((peers, total), 1) // each == iota((peers, total), 0))
    full = dot(narrow(send >> 5), pick) * 32.0 + dot(narrow(send & 31), pick)
    mine = jnp.where(iota((each, total), 0) == iota((each, total), 1) % each, full, 0.0)
    return jnp.sum(mine, axis=0, keepdims=True).astype(jnp.int32)


def gather_matrix(column, rows):
    return one_hot(iota((column.shape[0], rows), 1) == column)


def scatter_matrix(row, rows, first=0):
    return one_hot(iota((rows, row.shape[1]), 0) + first == row)


def put_pieces(ref, tile, rows):
    for half in range(2):
        at = slice((tile + half) * TILE, (tile + half + 1) * TILE)
        ref[:, at, :] = rows[:, half * HALF : (half + 1) * HALF].reshape(ref.shape[0], TILE, HALF)


def get_pieces(ref, tile):
    halves = []
    for half in range(2):
        at = slice((tile + half) * TILE, (tile + half + 1) * TILE)
        halves.append(ref[:, at, :].reshape(ref.shape[0] * TILE, HALF))
    return jnp.concatenate(halves, axis=1)


def term_tiles(rows, width, per_peer):
    across = width // HALF
    return [
        (t // per_peer, t % per_peer, (t // across) * TILE, (t % across) * HALF)
        for t in range(rows // TILE * across)
    ]


class Far:
    def __init__(self, source, here, sem):
        self.here = here
        self.copy = pltpu.make_async_copy(source, here, sem)
        self.shape = here.shape
        self.copy.start()
        self.waiting = True

    def __getitem__(self, at):
        if self.waiting:
            self.copy.wait()
            self.waiting = False
        return self.here[at]


class FarOut:
    def __init__(self, target, here, sem):
        self.here = here
        self.copy = pltpu.make_async_copy(here, target, sem)
        self.shape = here.shape

    def __setitem__(self, at, value):
        self.here[at] = value

    def __getitem__(self, at):
        return self.here[at]

    def send(self):
        self.copy.start()


def sds(shape, dtype):
    return jax.ShapeDtypeStruct(shape, dtype)


def call(body, out, args, where, flops=0, name=None):
    many = isinstance(out, tuple)
    outs = out if many else (out,)
    every = list(args) + list(outs)
    spaces, staged, shapes = [], [], []
    for value, mark in zip(every, where, strict=True):
        if mark == "v":
            spaces.append(pl.BlockSpec(memory_space=pltpu.VMEM))
        elif mark == "s":
            spaces.append(pl.BlockSpec(memory_space=pltpu.SMEM))
        else:
            spaces.append(pl.BlockSpec(memory_space=pltpu.HBM))
            shape = value.shape if mark == "f" else (mark,) + value.shape[1:]
            shapes.append(pltpu.VMEM(shape, value.dtype))
        staged.append(mark not in ("v", "s"))
    count = len(shapes)

    def kernel(*refs):
        given = list(refs[: len(every)])
        scratch = list(refs[len(every) : len(every) + count])
        sems = refs[-1] if count else None
        used = 0
        late = []
        for k, far in enumerate(staged):
            if not far:
                continue
            here = scratch[used]
            if k < len(args):
                source = given[k] if where[k] == "f" else given[k].at[pl.ds(0, where[k])]
                given[k] = Far(source, here, sems.at[used])
            else:
                given[k] = FarOut(given[k], here, sems.at[used])
                late.append(given[k])
            used += 1
        body(*given)
        for item in given[: len(args)]:
            if isinstance(item, Far) and item.waiting:
                item.copy.wait()
        for item in late:
            item.copy.wait()

    moved = sum(v.size * v.dtype.itemsize for v in every)
    return pl.pallas_call(
        kernel,
        out_shape=out,
        in_specs=spaces[: len(args)],
        out_specs=tuple(spaces[len(args) :]) if many else spaces[-1],
        scratch_shapes=shapes + ([pltpu.SemaphoreType.DMA((count,))] if count else []),
        compiler_params=pltpu.CompilerParams(vmem_limit_bytes=ROOM),
        cost_estimate=pl.CostEstimate(flops=flops, bytes_accessed=moved, transcendentals=0),
        name=name,
    )(*args)


def first_kernel(send, x, d, o):
    chosen = gather_matrix(index_column(send[...]), x.shape[0])
    put_pieces(o, 2, d[...])
    put_pieces(o, 0, dot(chosen, x[...]).astype(BF16))


def adjacency_kernel(counts, ib, ob, it, ot, x, master, mirror, part_master, part_mirror, mirror_mirror):
    masters = x.shape[0] // BLOCK
    mirrors = mirror.shape[1] // BLOCK
    master.here[...] = jnp.zeros(master.shape, BF16)
    mirror.here[...] = jnp.zeros(mirror.shape, BF16)

    def place(tiles, table, count, into, first):
        def step(k, carry):
            @pl.when(k < count)
            def _():
                dst = table[0, k]
                dst = jnp.where(dst >= masters, dst - masters, dst + mirrors)
                src = table[1, k] - first
                rows = pl.ds(pl.multiple_of(dst * BLOCK, BLOCK), BLOCK)
                cols = pl.ds(pl.multiple_of(src * BLOCK, BLOCK), BLOCK)
                into[rows, cols] = tiles[k]

            return carry

        lax.fori_loop(0, tiles.shape[0], step, 0)

    it.copy.wait()
    it.waiting = False
    ot.copy.wait()
    ot.waiting = False
    place(it.here, ib, counts[0, 0], master.here, 0)
    place(ot.here, ob, counts[0, 1], mirror.here, masters)
    master.send()
    mirror.send()
    size = mirrors * BLOCK
    mirror_mirror[...] = mirror[:size, :]
    part_mirror[...] = dot(master[:size, :], x[...])
    part_master[...] = dot(master[size:, :], x[...])
    part_master.send()


def mirror_part_kernel(part, a, got, o):
    rows = part[...] + dot(a[...], get_pieces(got, 0))
    put_pieces(o, 0, rows.astype(BF16))


def master_part_kernel(part, a, got, x, w, send, d, p, z, g):
    m = a.shape[1]
    z[...] = dot(x[...], w[...])
    z.send()
    p[...] = part[...] + dot(a[m:, :], get_pieces(got, 0))
    p.send()
    spread = scatter_matrix(index_row(send[...]), x.shape[0])
    g[...] = d[...].astype(F32) + dot(spread, get_pieces(got, 2))
    g.send()


def dense_kernel(send, deg, p, z, g, got, w, x, out, dz, davg, pick):
    rows, width = p.shape
    peers = pick.shape[0]
    row = index_row(send[...])
    pieces = get_pieces(got, 0)
    step = 256
    means = []
    for first in range(0, rows, step):
        at = slice(first, first + step)
        degree = deg[at, :]
        total = p[at, :] + dot(scatter_matrix(row, step, first), pieces)
        mean = (total / degree).astype(BF16)
        means.append(mean)
        zz = z[at, :] + dot(mean, w[...])
        s = jax.nn.sigmoid(zz)
        u = zz * s
        scale = lax.rsqrt(jnp.mean(u * u, axis=1, keepdims=True) + 1e-05)
        n = u * scale
        out[at, :] = n.astype(BF16)
        gg = g[at, :]
        du = scale * (gg - n * jnp.mean(gg * n, axis=1, keepdims=True))
        dzz = (du * (s * (1.0 + zz * (1.0 - s)))).astype(BF16)
        dz[at, :] = dzz
        davg[at, :] = (dot(dzz, w[...], NT) / degree).astype(BF16)
    out.send()
    dz.send()
    davg.send()
    chosen = gather_matrix(index_column(send[...]), rows)
    put_pieces(pick, 0, dot(chosen, davg[...]).astype(BF16))
    put_pieces(pick, 2, dot(chosen, out[...]).astype(BF16))
    terms = (dot(x[...], dz[...], TN).astype(BF16), dot(jnp.concatenate(means, axis=0), dz[...], TN).astype(BF16))
    per_peer = pick.shape[1] // TILE - 4
    tiles = term_tiles(2 * width, width, per_peer)
    for peer, place, first, column in tiles:
        term = terms[first // width][first % width : first % width + TILE, column : column + HALF]
        pick[peer, (4 + place) * TILE : (5 + place) * TILE, :] = term
    for t in range(len(tiles), peers * per_peer):
        place = t % per_peer
        pick[t // per_peer, (4 + place) * TILE : (5 + place) * TILE, :] = jnp.zeros((TILE, HALF), BF16)


def back_kernel(dz, w, davg, am, ar, o, r):
    m = ar.shape[1]
    r[...] = dot(ar[m:, :], davg[...], TN)
    o[...] = dot(dz[...], w[...], NT) + dot(am[m:, :], davg[...], TN)
    o.send()


def total_kernel(got, o):
    total = jnp.sum(got[:, 4 * TILE :, :].astype(F32), axis=0).astype(BF16)
    o[...] = jnp.broadcast_to(total[None], o.shape)


def mirror_back_kernel(back, a, got, o):
    put_pieces(o, 0, (back[...] + dot(a[...], get_pieces(got, 0), TN)).astype(BF16))


def master_back_kernel(back, a, got, o, out):
    o[...] = back[...] + dot(a[...], get_pieces(got, 0), TN)
    out[...] = get_pieces(got, 2)
    out.send()


def pack_kernel(rows, got, o):
    o[:, : 2 * TILE, :] = rows[...]
    total = jnp.sum(got[...].astype(F32), axis=0).astype(BF16)
    o[:, 2 * TILE :, :] = jnp.broadcast_to(total[None], (o.shape[0],) + total.shape)


def grad_kernel(send, back, got, o, w_self, w_neigh):
    width = w_self.shape[0]
    for peer, place, first, column in term_tiles(2 * width, width, got.shape[1] // TILE - 2):
        into = (w_self, w_neigh)[first // width]
        rows = slice(first % width, first % width + TILE)
        into[rows, column : column + HALF] = got[peer, (2 + place) * TILE : (3 + place) * TILE, :].astype(F32)
    w_self.send()
    w_neigh.send()
    spread = scatter_matrix(index_row(send[...]), o.shape[0])
    o[...] = (back[...] + dot(spread, get_pieces(got, 0))).astype(BF16)
    o.send()


def on_device(
    dom,
    grp,
    features,
    w_self,
    w_neigh,
    degree,
    send_rows,
    inner_tiles,
    inner_blocks,
    outer_tiles,
    outer_blocks,
    tile_counts,
    d_out,
    d_mirror,
):
    rows, width = features.shape
    peers, each = send_rows.shape
    mirrors = peers * each
    slots = rows + mirrors
    mm = 2 * width
    groups = lax.axis_size(grp)
    tiles = 2 * width * width // (TILE * HALF)
    per_peer = -(-tiles // peers)

    def exchange(values, axis):
        return lax.all_to_all(values, axis, split_axis=0, concat_axis=0, tiled=True)

    def parcel(count, many=peers):
        return sds((many, count * TILE, HALF), BF16)

    def wide(count, dtype=F32):
        return sds((count, width), dtype)

    send = send_rows.T
    degree_col = degree[:, None]

    got_h = exchange(
        call(first_kernel, parcel(4), (send, features, d_mirror), "vffv", mm * mirrors * rows, "pick_h"), dom
    )
    a_master, a_mirror, part_master, part_mirror, a_corner = call(
        adjacency_kernel,
        (sds((slots, rows), BF16), sds((slots, mirrors), BF16), wide(rows), wide(mirrors), sds((mirrors, mirrors), BF16)),
        (tile_counts, inner_blocks.T, outer_blocks.T, inner_tiles, outer_tiles, features),
        "sss" + "fff" + "fffvv",
        mm * slots * rows,
        "adjacency",
    )
    mirror_part = call(
        mirror_part_kernel, parcel(2), (part_mirror, a_corner, got_h), "vvvv", mm * mirrors * mirrors, "mirror_part"
    )
    got_part = exchange(mirror_part, dom)
    p_master, z_self, g_out = call(
        master_part_kernel,
        (wide(rows),) * 3,
        (part_master, a_mirror, got_h, features, w_self, send, d_out),
        "ffvfvvf" + "fff",
        mm * rows * (2 * mirrors + width),
        "master_part",
    )
    out, dz, d_avg, pick_g = call(
        dense_kernel,
        (wide(rows, BF16),) * 3 + (parcel(4 + per_peer),),
        (send, degree_col, p_master, z_self, g_out, got_part, w_neigh, features),
        "vffffvvf" + "fffv",
        mm * rows * (2 * mirrors + 4 * width),
        "dense",
    )
    got_g = exchange(pick_g, dom)
    back, back_mirror = call(
        back_kernel,
        (wide(rows), wide(mirrors)),
        (dz, w_self, d_avg, a_master, a_mirror),
        "fvfff" + "fv",
        mm * rows * (width + slots),
        "back",
    )
    got_terms = exchange(call(total_kernel, parcel(per_peer, groups), (got_g,), "vv", name="totals"), grp)
    mirror_back = call(
        mirror_back_kernel, parcel(2), (back_mirror, a_corner, got_g), "vvvv", mm * mirrors * mirrors, "mirror_back"
    )
    back, mirror_out = call(
        master_back_kernel,
        (wide(rows), wide(mirrors, BF16)),
        (back, a_master, got_g),
        ("f", mirrors, "v", "v", "f"),
        mm * rows * mirrors,
        "master_back",
    )
    got_back = exchange(call(pack_kernel, parcel(2 + per_peer), (mirror_back, got_terms), "vvv", name="pack"), dom)
    grad_h, grad_wself, grad_wneigh = call(
        grad_kernel,
        (wide(rows, BF16), wide(width), wide(width)),
        (send, back, got_back),
        "vvv" + "fff",
        mm * rows * mirrors,
        "grad",
    )
    return (out, mirror_out, grad_h, grad_wself, grad_wneigh)


def solution(mesh):
    names = ("dom", "grp")
    split = lambda rank: P(names, *([None] * (rank - 1)))
    in_specs = (
        split(2), P(), P(), split(1), split(2), split(3), split(2), split(3), split(2), split(2),
        split(2), split(2),
    )
    out_specs = (split(2), split(2), split(2), P(), P())
    return jax.shard_map(
        functools.partial(on_device, "dom", "grp"),
        mesh=mesh, in_specs=in_specs, out_specs=out_specs, check_vma=False,
    )
```

```python
import functools

import jax
import jax.numpy as jnp
from jax import lax
from jax.experimental import pallas as pl
from jax.experimental.pallas import tpu as pltpu
from jax.sharding import PartitionSpec as P

BLOCK = 128
HALF = 128
TILE = 16
BF16 = jnp.bfloat16
F32 = jnp.float32
NN = (((1,), (0,)), ((), ()))
TN = (((0,), (0,)), ((), ()))
NT = (((1,), (1,)), ((), ()))
ROOM = 62_500_000
LITTLE = 8_000_000


def dot(a, b, dims=NN):
    return lax.dot_general(a, b, dims, preferred_element_type=F32)


def one_hot(mask):
    return jnp.where(mask, 1.0, 0.0).astype(BF16)


def iota(shape, dim):
    return lax.broadcasted_iota(jnp.int32, shape, dim)


def narrow(value):
    return value.astype(F32).astype(BF16)


def index_column(send):
    each, peers = send.shape
    total = each * peers
    pick = one_hot(iota((total, peers), 0) // each == iota((total, peers), 1))
    full = dot(pick, narrow(send >> 5), NT) * 32.0 + dot(pick, narrow(send & 31), NT)
    mine = jnp.where(iota((total, each), 1) == iota((total, each), 0) % each, full, 0.0)
    return jnp.sum(mine, axis=1, keepdims=True).astype(jnp.int32)


def index_row(send):
    each, peers = send.shape
    total = each * peers
    pick = one_hot(iota((peers, total), 1) // each == iota((peers, total), 0))
    full = dot(narrow(send >> 5), pick) * 32.0 + dot(narrow(send & 31), pick)
    mine = jnp.where(iota((each, total), 0) == iota((each, total), 1) % each, full, 0.0)
    return jnp.sum(mine, axis=0, keepdims=True).astype(jnp.int32)


def gather_matrix(column, rows):
    return one_hot(iota((column.shape[0], rows), 1) == column)


def scatter_matrix(row, rows, first=0):
    return one_hot(iota((rows, row.shape[1]), 0) + first == row)


def put_pieces(ref, tile, rows):
    for half in range(2):
        at = slice((tile + half) * TILE, (tile + half + 1) * TILE)
        ref[:, at, :] = rows[:, half * HALF : (half + 1) * HALF].reshape(ref.shape[0], TILE, HALF)


def get_pieces(ref, tile):
    halves = []
    for half in range(2):
        at = slice((tile + half) * TILE, (tile + half + 1) * TILE)
        halves.append(ref[:, at, :].reshape(ref.shape[0] * TILE, HALF))
    return jnp.concatenate(halves, axis=1)


class Far:
    def __init__(self, source, here, sem):
        self.here = here
        self.copy = pltpu.make_async_copy(source, here, sem)
        self.shape = here.shape
        self.copy.start()
        self.waiting = True

    def __getitem__(self, at):
        if self.waiting:
            self.copy.wait()
            self.waiting = False
        return self.here[at]


class FarOut:
    def __init__(self, target, here, sem):
        self.here = here
        self.copy = pltpu.make_async_copy(here, target, sem)
        self.shape = here.shape

    def __setitem__(self, at, value):
        self.here[at] = value

    def __getitem__(self, at):
        return self.here[at]

    def send(self):
        self.copy.start()


def sds(shape, dtype):
    return jax.ShapeDtypeStruct(shape, dtype)


def call(body, out, args, where, flops=0, name=None, room=ROOM):
    many = isinstance(out, tuple)
    outs = out if many else (out,)
    every = list(args) + list(outs)
    spaces, staged, shapes = [], [], []
    for value, mark in zip(every, where, strict=True):
        if mark == "v":
            spaces.append(pl.BlockSpec(memory_space=pltpu.VMEM))
        elif mark == "x":
            spaces.append(pl.BlockSpec(memory_space=pl.ANY))
        elif mark == "s":
            spaces.append(pl.BlockSpec(memory_space=pltpu.SMEM))
        else:
            spaces.append(pl.BlockSpec(memory_space=pltpu.HBM))
            shape = value.shape if mark == "f" else (mark,) + value.shape[1:]
            shapes.append(pltpu.VMEM(shape, value.dtype))
        staged.append(mark not in ("v", "s", "x"))
    count = len(shapes)

    def kernel(*refs):
        given = list(refs[: len(every)])
        scratch = list(refs[len(every) : len(every) + count])
        sems = refs[-1] if count else None
        used = 0
        late = []
        for k, far in enumerate(staged):
            if not far:
                continue
            here = scratch[used]
            if k < len(args):
                source = given[k] if where[k] == "f" else given[k].at[pl.ds(0, where[k])]
                given[k] = Far(source, here, sems.at[used])
            else:
                given[k] = FarOut(given[k], here, sems.at[used])
                late.append(given[k])
            used += 1
        body(*given)
        for item in given[: len(args)]:
            if isinstance(item, Far) and item.waiting:
                item.copy.wait()
        for item in late:
            item.copy.wait()

    moved = sum(v.size * v.dtype.itemsize for v in every)
    return pl.pallas_call(
        kernel,
        out_shape=out,
        in_specs=spaces[: len(args)],
        out_specs=tuple(spaces[len(args) :]) if many else spaces[-1],
        scratch_shapes=shapes + ([pltpu.SemaphoreType.DMA((count,))] if count else []),
        compiler_params=pltpu.CompilerParams(vmem_limit_bytes=room),
        cost_estimate=pl.CostEstimate(flops=flops, bytes_accessed=moved, transcendentals=0),
        name=name,
    )(*args)


def first_kernel(send, x, d, o):
    chosen = gather_matrix(index_column(send[...]), x.shape[0])
    put_pieces(o, 2, d[...])
    put_pieces(o, 0, dot(chosen, x[...]).astype(BF16))


def adjacency_kernel(counts, ib, ob, it, ot, x, master, mirror, part_master, part_mirror, mirror_mirror):
    masters = x.shape[0] // BLOCK
    mirrors = mirror.shape[1] // BLOCK
    master.here[...] = jnp.zeros(master.shape, BF16)
    mirror.here[...] = jnp.zeros(mirror.shape, BF16)

    def place(tiles, table, count, into, first):
        def step(k, carry):
            @pl.when(k < count)
            def _():
                dst = table[0, k]
                dst = jnp.where(dst >= masters, dst - masters, dst + mirrors)
                src = table[1, k] - first
                rows = pl.ds(pl.multiple_of(dst * BLOCK, BLOCK), BLOCK)
                cols = pl.ds(pl.multiple_of(src * BLOCK, BLOCK), BLOCK)
                into[rows, cols] = tiles[k]

            return carry

        lax.fori_loop(0, tiles.shape[0], step, 0)

    it.copy.wait()
    it.waiting = False
    ot.copy.wait()
    ot.waiting = False
    place(it.here, ib, counts[0, 0], master.here, 0)
    place(ot.here, ob, counts[0, 1], mirror.here, masters)
    master.send()
    mirror.send()
    size = mirrors * BLOCK
    mirror_mirror[...] = mirror[:size, :]
    part_mirror[...] = dot(master[:size, :], x[...])
    part_master[...] = dot(master[size:, :], x[...])
    part_master.send()


def mirror_part_kernel(part, a, got, o):
    rows = part[...] + dot(a[...], get_pieces(got, 0))
    put_pieces(o, 0, rows.astype(BF16))


def master_part_kernel(part, a, got, x, w, send, d, p, z, g):
    m = a.shape[1]
    z[...] = dot(x[...], w[...])
    z.send()
    p[...] = part[...] + dot(a[m:, :], get_pieces(got, 0))
    p.send()
    spread = scatter_matrix(index_row(send[...]), x.shape[0])
    g[...] = d[...].astype(F32) + dot(spread, get_pieces(got, 2))
    g.send()


def dense_kernel(send, deg, p, z, g, got, w, avg, out, dz, davg, pick):
    rows, width = p.shape
    row = index_row(send[...])
    pieces = get_pieces(got, 0)
    step = 256
    for first in range(0, rows, step):
        at = slice(first, first + step)
        degree = deg[at, :]
        total = p[at, :] + dot(scatter_matrix(row, step, first), pieces)
        mean = (total / degree).astype(BF16)
        avg[at, :] = mean
        zz = z[at, :] + dot(mean, w[...])
        s = jax.nn.sigmoid(zz)
        u = zz * s
        scale = lax.rsqrt(jnp.mean(u * u, axis=1, keepdims=True) + 1e-05)
        n = u * scale
        out[at, :] = n.astype(BF16)
        gg = g[at, :]
        du = scale * (gg - n * jnp.mean(gg * n, axis=1, keepdims=True))
        dzz = (du * (s * (1.0 + zz * (1.0 - s)))).astype(BF16)
        dz[at, :] = dzz
        davg[at, :] = (dot(dzz, w[...], NT) / degree).astype(BF16)
    out.send()
    dz.send()
    davg.send()
    avg.send()
    chosen = gather_matrix(index_column(send[...]), rows)
    put_pieces(pick, 0, dot(chosen, davg[...]).astype(BF16))
    put_pieces(pick, 2, dot(chosen, out[...]).astype(BF16))


def weight_kernel(x, avg, dz, after, o):
    half = o.shape[0] // 2
    put_pieces(o.at[:half], 0, dot(x[...], dz[...], TN).astype(BF16))
    put_pieces(o.at[half:], 0, dot(avg[...], dz[...], TN).astype(BF16))


def back_kernel(dz, w, davg, am, ar, o, r):
    m = ar.shape[1]
    r[...] = dot(ar[m:, :], davg[...], TN)
    o[...] = dot(dz[...], w[...], NT) + dot(am[m:, :], davg[...], TN)
    o.send()


def mirror_back_kernel(back, a, got, o):
    put_pieces(o, 0, (back[...] + dot(a[...], get_pieces(got, 0), TN)).astype(BF16))


def master_back_kernel(back, a, got, o, out):
    o[...] = back[...] + dot(a[...], get_pieces(got, 0), TN)
    o.send()
    out[...] = get_pieces(got, 2)
    out.send()


def pack_kernel(rows, got, o):
    o[:, : 2 * TILE, :] = rows[...]
    total = jnp.sum(got[...].astype(F32), axis=0).astype(BF16)
    o[:, 2 * TILE :, :] = jnp.broadcast_to(total[None], (o.shape[0],) + total.shape)


def share_kernel(got, o):
    total = jnp.sum(got[:, 2 * TILE :, :].astype(F32), axis=0).astype(BF16)
    o[...] = jnp.broadcast_to(total[None], o.shape)


def grad_kernel(send, back, got, o):
    spread = scatter_matrix(index_row(send[...]), o.shape[0])
    o[...] = (back[...] + dot(spread, get_pieces(got, 0))).astype(BF16)
    o.send()


def widen_kernel(got, w_self, w_neigh):
    half = got.shape[0] // 2
    w_self[...] = get_pieces(got.at[:half], 0).astype(F32)
    w_self.send()
    w_neigh[...] = get_pieces(got.at[half:], 0).astype(F32)
    w_neigh.send()


def on_device(
    dom,
    grp,
    features,
    w_self,
    w_neigh,
    degree,
    send_rows,
    inner_tiles,
    inner_blocks,
    outer_tiles,
    outer_blocks,
    tile_counts,
    d_out,
    d_mirror,
):
    rows, width = features.shape
    peers, each = send_rows.shape
    mirrors = peers * each
    slots = rows + mirrors
    mm = 2 * width
    groups = lax.axis_size(grp)
    def exchange(values, axis):
        return lax.all_to_all(values, axis, split_axis=0, concat_axis=0, tiled=True)

    def parcel(count, many=peers):
        return sds((many, count * TILE, HALF), BF16)

    def wide(count, dtype=F32):
        return sds((count, width), dtype)

    send = send_rows.T
    degree_col = degree[:, None]

    got_h = exchange(
        call(first_kernel, parcel(4), (send, features, d_mirror), "vffv", mm * mirrors * rows, "pick_h"), dom
    )
    a_master, a_mirror, part_master, part_mirror, a_corner = call(
        adjacency_kernel,
        (sds((slots, rows), BF16), sds((slots, mirrors), BF16), wide(rows), wide(mirrors), sds((mirrors, mirrors), BF16)),
        (tile_counts, inner_blocks.T, outer_blocks.T, inner_tiles, outer_tiles, features),
        "sss" + "fff" + "fffvv",
        mm * slots * rows,
        "adjacency",
    )
    mirror_part = call(
        mirror_part_kernel, parcel(2), (part_mirror, a_corner, got_h), "vvvv", mm * mirrors * mirrors, "mirror_part", ROOM
    )
    got_part = exchange(mirror_part, dom)
    p_master, z_self, g_out = call(
        master_part_kernel,
        (wide(rows),) * 3,
        (part_master, a_mirror, got_h, features, w_self, send, d_out),
        "ffvfvvf" + "fff",
        mm * rows * (2 * mirrors + width),
        "master_part",
    )
    avg, out, dz, d_avg, pick_g = call(
        dense_kernel,
        (wide(rows, BF16),) * 4 + (parcel(4),),
        (send, degree_col, p_master, z_self, g_out, got_part, w_neigh),
        "vffffvv" + "ffffv",
        mm * rows * (2 * mirrors + 2 * width),
        "dense",
    )
    got_g = exchange(pick_g, dom)
    back, back_mirror = call(
        back_kernel,
        (wide(rows), wide(mirrors)),
        (dz, w_self, d_avg, a_master, a_mirror),
        "fvfff" + "fv",
        mm * rows * (width + slots),
        "back",
    )
    terms = call(
        weight_kernel, parcel(2, groups), (features, avg, dz, back_mirror), "fff" + "x" + "v", 2 * mm * rows * width, "weights"
    )
    got_terms = exchange(terms, grp)
    mirror_back = call(
        mirror_back_kernel,
        parcel(2),
        (back_mirror, a_corner, got_g),
        "vvvv",
        mm * mirrors * mirrors,
        "mirror_back",
        LITTLE,
    )
    packed = call(pack_kernel, parcel(4), (mirror_back, got_terms), "vvv", 0, "pack", LITTLE)
    got_back = exchange(packed, dom)
    back, mirror_out = call(
        master_back_kernel,
        (wide(rows), wide(mirrors, BF16)),
        (back, a_master, got_g),
        ("f", mirrors, "v", "f", "f"),
        mm * rows * mirrors,
        "master_back",
    )
    shared = call(share_kernel, parcel(2, groups), (got_back,), "vv", 0, "share", LITTLE)
    totals = exchange(shared, grp)
    grad_h = call(
        grad_kernel, wide(rows, BF16), (send, back, got_back), "vfv" + "f", mm * rows * mirrors, "grad"
    )
    grad_wself, grad_wneigh = call(
        widen_kernel, (wide(width),) * 2, (totals,), "vff", 0, "widen", LITTLE
    )
    return (out, mirror_out, grad_h, grad_wself, grad_wneigh)


def solution(mesh):
    names = ("dom", "grp")
    split = lambda rank: P(names, *([None] * (rank - 1)))
    in_specs = (
        split(2), P(), P(), split(1), split(2), split(3), split(2), split(3), split(2), split(2),
        split(2), split(2),
    )
    out_specs = (split(2), split(2), split(2), P(), P())
    return jax.shard_map(
        functools.partial(on_device, "dom", "grp"),
        mesh=mesh, in_specs=in_specs, out_specs=out_specs, check_vma=False,
    )
```

```python
import functools

import jax
import jax.numpy as jnp
from jax import lax
from jax.experimental import pallas as pl
from jax.experimental.pallas import tpu as pltpu
from jax.sharding import PartitionSpec as P

BLOCK = 128
HALF = 128
TILE = 16
BF16 = jnp.bfloat16
F32 = jnp.float32
NN = (((1,), (0,)), ((), ()))
TN = (((0,), (0,)), ((), ()))
NT = (((1,), (1,)), ((), ()))
ROOM = 62_500_000
LITTLE = 8_000_000
PARTS = 4


def dot(a, b, dims=NN):
    return lax.dot_general(a, b, dims, preferred_element_type=F32)


def one_hot(mask):
    return jnp.where(mask, 1.0, 0.0).astype(BF16)


def iota(shape, dim):
    return lax.broadcasted_iota(jnp.int32, shape, dim)


def narrow(value):
    return value.astype(F32).astype(BF16)


def index_column(send):
    each, peers = send.shape
    total = each * peers
    pick = one_hot(iota((total, peers), 0) // each == iota((total, peers), 1))
    full = dot(pick, narrow(send >> 5), NT) * 32.0 + dot(pick, narrow(send & 31), NT)
    mine = jnp.where(iota((total, each), 1) == iota((total, each), 0) % each, full, 0.0)
    return jnp.sum(mine, axis=1, keepdims=True).astype(jnp.int32)


def index_row(send):
    each, peers = send.shape
    total = each * peers
    pick = one_hot(iota((peers, total), 1) // each == iota((peers, total), 0))
    full = dot(narrow(send >> 5), pick) * 32.0 + dot(narrow(send & 31), pick)
    mine = jnp.where(iota((each, total), 0) == iota((each, total), 1) % each, full, 0.0)
    return jnp.sum(mine, axis=0, keepdims=True).astype(jnp.int32)


def gather_matrix(column, rows):
    return one_hot(iota((column.shape[0], rows), 1) == column)


def scatter_matrix(row, rows, first=0):
    return one_hot(iota((rows, row.shape[1]), 0) + first == row)


def put_pieces(ref, tile, rows):
    for half in range(2):
        at = slice((tile + half) * TILE, (tile + half + 1) * TILE)
        ref[:, at, :] = rows[:, half * HALF : (half + 1) * HALF].reshape(ref.shape[0], TILE, HALF)


def get_pieces(ref, tile):
    halves = []
    for half in range(2):
        at = slice((tile + half) * TILE, (tile + half + 1) * TILE)
        halves.append(ref[:, at, :].reshape(ref.shape[0] * TILE, HALF))
    return jnp.concatenate(halves, axis=1)


class Far:
    def __init__(self, source, here, sem):
        self.here = here
        self.copy = pltpu.make_async_copy(source, here, sem)
        self.shape = here.shape
        self.copy.start()
        self.waiting = True

    def __getitem__(self, at):
        if self.waiting:
            self.copy.wait()
            self.waiting = False
        return self.here[at]


class FarOut:
    def __init__(self, target, here, sem):
        self.here = here
        self.copy = pltpu.make_async_copy(here, target, sem)
        self.shape = here.shape

    def __setitem__(self, at, value):
        self.here[at] = value

    def __getitem__(self, at):
        return self.here[at]

    def send(self):
        self.copy.start()


class Parts:
    def __init__(self, far, here, sems, first, into):
        step = here.shape[0] // PARTS
        self.here, self.shape, self.copies, self.waiting = here, here.shape, [], [into] * PARTS
        for k in range(PARTS):
            at = pl.ds(k * step, step)
            ends = (far.at[at], here.at[at]) if into else (here.at[at], far.at[at])
            self.copies.append(pltpu.make_async_copy(*ends, sems.at[first + k]))
        self.step = step

    def start(self, k):
        self.copies[k].start()

    def get(self, k):
        if self.waiting[k]:
            self.copies[k].wait()
            self.waiting[k] = False
        return self.here[k * self.step : (k + 1) * self.step, :]

    def put(self, k, value):
        self.here[k * self.step : (k + 1) * self.step, :] = value
        self.copies[k].start()


def sds(shape, dtype):
    return jax.ShapeDtypeStruct(shape, dtype)


def call(body, out, args, where, flops=0, name=None, room=ROOM):
    many = isinstance(out, tuple)
    outs = out if many else (out,)
    every = list(args) + list(outs)
    spaces, staged, shapes = [], [], []
    for value, mark in zip(every, where, strict=True):
        if mark == "v":
            spaces.append(pl.BlockSpec(memory_space=pltpu.VMEM))
        elif mark == "x":
            spaces.append(pl.BlockSpec(memory_space=pl.ANY))
        elif mark == "s":
            spaces.append(pl.BlockSpec(memory_space=pltpu.SMEM))
        else:
            spaces.append(pl.BlockSpec(memory_space=pltpu.HBM))
            shape = value.shape if mark in ("f", "c") else (mark,) + value.shape[1:]
            shapes.append(pltpu.VMEM(shape, value.dtype))
        staged.append(mark not in ("v", "s", "x"))
    count = len(shapes)

    lengths = [PARTS if mark == "c" else 1 for mark, far in zip(where, staged) if far]

    def kernel(*refs):
        given = list(refs[: len(every)])
        scratch = list(refs[len(every) : len(every) + count])
        sems = refs[-1] if count else None
        used, at = 0, 0
        parts, late = [], []
        for k, far in enumerate(staged):
            if not far:
                continue
            here = scratch[used]
            if where[k] == "c":
                given[k] = Parts(given[k], here, sems, at, k < len(args))
                parts.append(given[k])
            elif k < len(args):
                source = given[k] if where[k] == "f" else given[k].at[pl.ds(0, where[k])]
                given[k] = Far(source, here, sems.at[at])
            else:
                given[k] = FarOut(given[k], here, sems.at[at])
                late.append(given[k])
            at += lengths[used]
            used += 1
        for k in range(PARTS):
            for item in parts:
                if item.waiting[k]:
                    item.start(k)
        body(*given)
        for item in given[: len(args)]:
            if isinstance(item, Far) and item.waiting:
                item.copy.wait()
        for item in late:
            item.copy.wait()
        for item in given[len(args) :]:
            if isinstance(item, Parts):
                for copy in item.copies:
                    copy.wait()

    moved = sum(v.size * v.dtype.itemsize for v in every)
    return pl.pallas_call(
        kernel,
        out_shape=out,
        in_specs=spaces[: len(args)],
        out_specs=tuple(spaces[len(args) :]) if many else spaces[-1],
        scratch_shapes=shapes + ([pltpu.SemaphoreType.DMA((sum(lengths),))] if count else []),
        compiler_params=pltpu.CompilerParams(vmem_limit_bytes=room),
        cost_estimate=pl.CostEstimate(flops=flops, bytes_accessed=moved, transcendentals=0),
        name=name,
    )(*args)


def first_kernel(send, x, d, o):
    chosen = gather_matrix(index_column(send[...]), x.shape[0])
    put_pieces(o, 2, d[...])
    put_pieces(o, 0, dot(chosen, x[...]).astype(BF16))


def adjacency_kernel(counts, ib, ob, it, ot, x, master, mirror, part_master, part_mirror, mirror_mirror):
    masters = x.shape[0] // BLOCK
    mirrors = mirror.shape[1] // BLOCK
    master.here[...] = jnp.zeros(master.shape, BF16)
    mirror.here[...] = jnp.zeros(mirror.shape, BF16)

    def place(tiles, table, count, into, first):
        def step(k, carry):
            @pl.when(k < count)
            def _():
                dst = table[0, k]
                dst = jnp.where(dst >= masters, dst - masters, dst + mirrors)
                src = table[1, k] - first
                rows = pl.ds(pl.multiple_of(dst * BLOCK, BLOCK), BLOCK)
                cols = pl.ds(pl.multiple_of(src * BLOCK, BLOCK), BLOCK)
                into[rows, cols] = tiles[k]

            return carry

        lax.fori_loop(0, tiles.shape[0], step, 0)

    it.copy.wait()
    it.waiting = False
    ot.copy.wait()
    ot.waiting = False
    place(it.here, ib, counts[0, 0], master.here, 0)
    place(ot.here, ob, counts[0, 1], mirror.here, masters)
    master.send()
    mirror.send()
    size = mirrors * BLOCK
    mirror_mirror[...] = mirror[:size, :]
    part_mirror[...] = dot(master[:size, :], x[...])
    part_master[...] = dot(master[size:, :], x[...])
    part_master.send()


def mirror_part_kernel(part, a, got, o):
    rows = part[...] + dot(a[...], get_pieces(got, 0))
    put_pieces(o, 0, rows.astype(BF16))


def master_part_kernel(part, a, got, x, w, send, d, p, z, g):
    m = a.shape[1]
    z[...] = dot(x[...], w[...])
    z.send()
    p[...] = part[...] + dot(a[m:, :], get_pieces(got, 0))
    p.send()
    spread = scatter_matrix(index_row(send[...]), x.shape[0])
    g[...] = d[...].astype(F32) + dot(spread, get_pieces(got, 2))
    g.send()


def dense_kernel(send, deg, p, z, g, got, w, avg, out, dz, davg, pick):
    rows, width = p.shape
    row = index_row(send[...])
    chosen = gather_matrix(index_column(send[...]), rows)
    pieces = get_pieces(got, 0)
    for k in range(PARTS):
        spread = scatter_matrix(row, p.step, k * p.step)
        share = 1.0 / deg.get(k)
        mean = ((p.get(k) + dot(spread, pieces)) * share).astype(BF16)
        avg.put(k, mean)
        zz = z.get(k) + dot(mean, w[...])
        s = jax.nn.sigmoid(zz)
        u = zz * s
        scale = lax.rsqrt(jnp.mean(u * u, axis=1, keepdims=True) + 1e-05)
        n = u * scale
        out.put(k, n.astype(BF16))
        gg = g.get(k)
        du = scale * (gg - n * jnp.mean(gg * n, axis=1, keepdims=True))
        dzz = (du * (s + u * (1.0 - s))).astype(BF16)
        dz.put(k, dzz)
        davg.put(k, (dot(dzz, w[...], NT) * share).astype(BF16))
    put_pieces(pick, 0, dot(chosen, davg.here[...]).astype(BF16))
    put_pieces(pick, 2, dot(chosen, out.here[...]).astype(BF16))


def weight_kernel(x, avg, dz, after, o):
    half = o.shape[0] // 2
    put_pieces(o.at[:half], 0, dot(x[...], dz[...], TN).astype(BF16))
    put_pieces(o.at[half:], 0, dot(avg[...], dz[...], TN).astype(BF16))


def back_kernel(dz, w, davg, am, ar, o, r):
    m = ar.shape[1]
    r[...] = dot(ar[m:, :], davg[...], TN)
    o[...] = dot(dz[...], w[...], NT) + dot(am[m:, :], davg[...], TN)
    o.send()


def mirror_back_kernel(back, a, got, o):
    put_pieces(o, 0, (back[...] + dot(a[...], get_pieces(got, 0), TN)).astype(BF16))


def master_back_kernel(back, a, got, o, out):
    o[...] = back[...] + dot(a[...], get_pieces(got, 0), TN)
    o.send()
    out[...] = get_pieces(got, 2)
    out.send()


def pack_kernel(rows, got, o):
    o[:, : 2 * TILE, :] = rows[...]
    total = jnp.sum(got[...].astype(F32), axis=0).astype(BF16)
    o[:, 2 * TILE :, :] = jnp.broadcast_to(total[None], (o.shape[0],) + total.shape)


def share_kernel(got, o):
    total = jnp.sum(got[:, 2 * TILE :, :].astype(F32), axis=0).astype(BF16)
    o[...] = jnp.broadcast_to(total[None], o.shape)


def grad_kernel(send, back, got, o):
    spread = scatter_matrix(index_row(send[...]), o.shape[0])
    o[...] = (back[...] + dot(spread, get_pieces(got, 0))).astype(BF16)
    o.send()


def widen_kernel(got, w_self, w_neigh):
    half = got.shape[0] // 2
    w_self[...] = get_pieces(got.at[:half], 0).astype(F32)
    w_self.send()
    w_neigh[...] = get_pieces(got.at[half:], 0).astype(F32)
    w_neigh.send()


def on_device(
    dom,
    grp,
    features,
    w_self,
    w_neigh,
    degree,
    send_rows,
    inner_tiles,
    inner_blocks,
    outer_tiles,
    outer_blocks,
    tile_counts,
    d_out,
    d_mirror,
):
    rows, width = features.shape
    peers, each = send_rows.shape
    mirrors = peers * each
    slots = rows + mirrors
    mm = 2 * width
    groups = lax.axis_size(grp)
    def exchange(values, axis):
        return lax.all_to_all(values, axis, split_axis=0, concat_axis=0, tiled=True)

    def parcel(count, many=peers):
        return sds((many, count * TILE, HALF), BF16)

    def wide(count, dtype=F32):
        return sds((count, width), dtype)

    send = send_rows.T
    degree_col = degree[:, None]

    got_h = exchange(
        call(first_kernel, parcel(4), (send, features, d_mirror), "vffv", mm * mirrors * rows, "pick_h"), dom
    )
    a_master, a_mirror, part_master, part_mirror, a_corner = call(
        adjacency_kernel,
        (sds((slots, rows), BF16), sds((slots, mirrors), BF16), wide(rows), wide(mirrors), sds((mirrors, mirrors), BF16)),
        (tile_counts, inner_blocks.T, outer_blocks.T, inner_tiles, outer_tiles, features),
        "sss" + "fff" + "fffvv",
        mm * slots * rows,
        "adjacency",
        40000000,
    )
    mirror_part = call(
        mirror_part_kernel, parcel(2), (part_mirror, a_corner, got_h), "vvvv", mm * mirrors * mirrors, "mirror_part", LITTLE
    )
    got_part = exchange(mirror_part, dom)
    p_master, z_self, g_out = call(
        master_part_kernel,
        (wide(rows),) * 3,
        (part_master, a_mirror, got_h, features, w_self, send, d_out),
        "ffvfvvf" + "fff",
        mm * rows * (2 * mirrors + width),
        "master_part",
    )
    avg, out, dz, d_avg, pick_g = call(
        dense_kernel,
        (wide(rows, BF16),) * 4 + (parcel(4),),
        (send, degree_col, p_master, z_self, g_out, got_part, w_neigh),
        "vccccvv" + "ccccv",
        mm * rows * (2 * mirrors + 2 * width),
        "dense",
    )
    got_g = exchange(pick_g, dom)
    back, back_mirror = call(
        back_kernel,
        (wide(rows), wide(mirrors)),
        (dz, w_self, d_avg, a_master, a_mirror),
        "fvfff" + "fv",
        mm * rows * (width + slots),
        "back",
    )
    terms = call(
        weight_kernel, parcel(2, groups), (features, avg, dz, back_mirror), "fff" + "x" + "v", 2 * mm * rows * width, "weights"
    )
    got_terms = exchange(terms, grp)
    mirror_back = call(
        mirror_back_kernel,
        parcel(2),
        (back_mirror, a_corner, got_g),
        "vvvv",
        mm * mirrors * mirrors,
        "mirror_back",
        LITTLE,
    )
    packed = call(pack_kernel, parcel(4), (mirror_back, got_terms), "vvv", 0, "pack", LITTLE)
    got_back = exchange(packed, dom)
    back, mirror_out = call(
        master_back_kernel,
        (wide(rows), wide(mirrors, BF16)),
        (back, a_master, got_g),
        ("f", mirrors, "v", "f", "f"),
        mm * rows * mirrors,
        "master_back",
    )
    shared = call(share_kernel, parcel(2, groups), (got_back,), "vv", 0, "share", LITTLE)
    totals = exchange(shared, grp)
    grad_h = call(
        grad_kernel, wide(rows, BF16), (send, back, got_back), "vfv" + "f", mm * rows * mirrors, "grad"
    )
    grad_wself, grad_wneigh = call(
        widen_kernel, (wide(width),) * 2, (totals,), "vff", 0, "widen", LITTLE
    )
    return (out, mirror_out, grad_h, grad_wself, grad_wneigh)


def solution(mesh):
    names = ("dom", "grp")
    split = lambda rank: P(names, *([None] * (rank - 1)))
    in_specs = (
        split(2), P(), P(), split(1), split(2), split(3), split(2), split(3), split(2), split(2),
        split(2), split(2),
    )
    out_specs = (split(2), split(2), split(2), P(), P())
    return jax.shard_map(
        functools.partial(on_device, "dom", "grp"),
        mesh=mesh, in_specs=in_specs, out_specs=out_specs, check_vma=False,
    )
```

```python
import functools

import jax
import jax.numpy as jnp
from jax import lax
from jax.experimental import pallas as pl
from jax.experimental.pallas import tpu as pltpu
from jax.sharding import PartitionSpec as P

BLOCK = 128
TILE = 16
BF16 = jnp.bfloat16
F32 = jnp.float32
NN = (((1,), (0,)), ((), ()))
TN = (((0,), (0,)), ((), ()))
NT = (((1,), (1,)), ((), ()))
ROOM = 62_500_000
LITTLE = 8_000_000


def dot(a, b, dims=NN):
    return lax.dot_general(a, b, dims, preferred_element_type=F32)


def one_hot(mask):
    return jnp.where(mask, 1.0, 0.0).astype(BF16)


def iota(shape, dim):
    return lax.broadcasted_iota(jnp.int32, shape, dim)


def narrow(value):
    return value.astype(F32).astype(BF16)


def index_column(send):
    each, peers = send.shape
    total = each * peers
    pick = one_hot(iota((total, peers), 0) // each == iota((total, peers), 1))
    full = dot(pick, narrow(send >> 5), NT) * 32.0 + dot(pick, narrow(send & 31), NT)
    mine = jnp.where(iota((total, each), 1) == iota((total, each), 0) % each, full, 0.0)
    return jnp.sum(mine, axis=1, keepdims=True).astype(jnp.int32)


def index_row(send):
    each, peers = send.shape
    total = each * peers
    pick = one_hot(iota((peers, total), 1) // each == iota((peers, total), 0))
    full = dot(narrow(send >> 5), pick) * 32.0 + dot(narrow(send & 31), pick)
    mine = jnp.where(iota((each, total), 0) == iota((each, total), 1) % each, full, 0.0)
    return jnp.sum(mine, axis=0, keepdims=True).astype(jnp.int32)


def gather_matrix(column, rows):
    return one_hot(iota((column.shape[0], rows), 1) == column)


def scatter_matrix(row, rows, first=0):
    return one_hot(iota((rows, row.shape[1]), 0) + first == row)


def put_pieces(ref, number, rows):
    ref[:, number * TILE : (number + 1) * TILE, :] = rows.reshape(ref.shape[0], TILE, ref.shape[2])


def get_pieces(ref, number):
    return ref[:, number * TILE : (number + 1) * TILE, :].reshape(ref.shape[0] * TILE, ref.shape[2])


class Far:
    def __init__(self, source, here, sem):
        self.here = here
        self.copy = pltpu.make_async_copy(source, here, sem)
        self.shape = here.shape
        self.copy.start()
        self.waiting = True

    def __getitem__(self, at):
        if self.waiting:
            self.copy.wait()
            self.waiting = False
        return self.here[at]


class FarOut:
    def __init__(self, target, here, sem):
        self.here = here
        self.copy = pltpu.make_async_copy(here, target, sem)
        self.shape = here.shape

    def __setitem__(self, at, value):
        self.here[at] = value

    def __getitem__(self, at):
        return self.here[at]

    def send(self):
        self.copy.start()


def sds(shape, dtype):
    return jax.ShapeDtypeStruct(shape, dtype)


def call(body, out, args, where, flops=0, name=None, room=ROOM):
    many = isinstance(out, tuple)
    outs = out if many else (out,)
    every = list(args) + list(outs)
    spaces, staged, shapes = [], [], []
    for value, mark in zip(every, where, strict=True):
        if mark == "v":
            spaces.append(pl.BlockSpec(memory_space=pltpu.VMEM))
        elif mark == "x":
            spaces.append(pl.BlockSpec(memory_space=pl.ANY))
        elif mark == "s":
            spaces.append(pl.BlockSpec(memory_space=pltpu.SMEM))
        else:
            spaces.append(pl.BlockSpec(memory_space=pltpu.HBM))
            shape = value.shape if mark == "f" else (mark,) + value.shape[1:]
            shapes.append(pltpu.VMEM(shape, value.dtype))
        staged.append(mark not in ("v", "s", "x"))
    count = len(shapes)

    def kernel(*refs):
        given = list(refs[: len(every)])
        scratch = list(refs[len(every) : len(every) + count])
        sems = refs[-1] if count else None
        used = 0
        late = []
        for k, far in enumerate(staged):
            if not far:
                continue
            here = scratch[used]
            if k < len(args):
                source = given[k] if where[k] == "f" else given[k].at[pl.ds(0, where[k])]
                given[k] = Far(source, here, sems.at[used])
            else:
                given[k] = FarOut(given[k], here, sems.at[used])
                late.append(given[k])
            used += 1
        body(*given)
        for item in given[: len(args)]:
            if isinstance(item, Far) and item.waiting:
                item.copy.wait()
        for item in late:
            item.copy.wait()

    moved = sum(v.size * v.dtype.itemsize for v in every)
    return pl.pallas_call(
        kernel,
        out_shape=out,
        in_specs=spaces[: len(args)],
        out_specs=tuple(spaces[len(args) :]) if many else spaces[-1],
        scratch_shapes=shapes + ([pltpu.SemaphoreType.DMA((count,))] if count else []),
        compiler_params=pltpu.CompilerParams(vmem_limit_bytes=room),
        cost_estimate=pl.CostEstimate(flops=flops, bytes_accessed=moved, transcendentals=0),
        name=name,
    )(*args)


def first_kernel(send, x, d, o):
    chosen = gather_matrix(index_column(send[...]), x.shape[0])
    put_pieces(o, 1, d[...])
    put_pieces(o, 0, dot(chosen, x[...]).astype(BF16))


def adjacency_kernel(counts, ib, ob, it, ot, x, master, mirror, part_master, part_mirror, mirror_mirror):
    masters = x.shape[0] // BLOCK
    mirrors = mirror.shape[1] // BLOCK
    master.here[...] = jnp.zeros(master.shape, BF16)
    mirror.here[...] = jnp.zeros(mirror.shape, BF16)

    def place(tiles, table, count, into, first):
        def step(k, carry):
            @pl.when(k < count)
            def _():
                dst = table[0, k]
                dst = jnp.where(dst >= masters, dst - masters, dst + mirrors)
                src = table[1, k] - first
                rows = pl.ds(pl.multiple_of(dst * BLOCK, BLOCK), BLOCK)
                cols = pl.ds(pl.multiple_of(src * BLOCK, BLOCK), BLOCK)
                into[rows, cols] = tiles[k]

            return carry

        lax.fori_loop(0, tiles.shape[0], step, 0)

    it.copy.wait()
    it.waiting = False
    ot.copy.wait()
    ot.waiting = False
    place(it.here, ib, counts[0, 0], master.here, 0)
    place(ot.here, ob, counts[0, 1], mirror.here, masters)
    master.send()
    mirror.send()
    size = mirrors * BLOCK
    mirror_mirror[...] = mirror[:size, :]
    part_mirror[...] = dot(master[:size, :], x[...])
    part_master[...] = dot(master[size:, :], x[...])
    part_master.send()


def mirror_part_kernel(part, a, got, o):
    rows = part[...] + dot(a[...], get_pieces(got, 0))
    put_pieces(o, 0, rows.astype(BF16))


def master_part_kernel(part, a, got, x, w, send, d, p, z, g):
    m = a.shape[1]
    z[...] = dot(x[...], w[...])
    z.send()
    p[...] = part[...] + dot(a[m:, :], get_pieces(got, 0))
    p.send()
    spread = scatter_matrix(index_row(send[...]), x.shape[0])
    g[...] = d[...].astype(F32) + dot(spread, get_pieces(got, 1))
    g.send()


def dense_kernel(send, deg, p, z, g, got, w, avg, out, dz, davg, pick):
    rows = p.shape[0]
    spread = scatter_matrix(index_row(send[...]), rows)
    chosen = gather_matrix(index_column(send[...]), rows)
    collected = dot(spread, get_pieces(got, 0))
    share = 1.0 / deg[...]
    mean = ((p[...] + collected) * share).astype(BF16)
    avg[...] = mean
    avg.send()
    zz = z[...] + dot(mean, w[...])
    s = jax.nn.sigmoid(zz)
    u = zz * s
    scale = lax.rsqrt(jnp.mean(u * u, axis=1, keepdims=True) + 1e-05)
    n = u * scale
    out[...] = n.astype(BF16)
    out.send()
    gg = g[...]
    du = scale * (gg - n * jnp.mean(gg * n, axis=1, keepdims=True))
    dz[...] = (du * (s + u * (1.0 - s))).astype(BF16)
    dz.send()
    davg[...] = (dot(dz[...], w[...], NT) * share).astype(BF16)
    davg.send()
    put_pieces(pick, 0, dot(chosen, davg[...]).astype(BF16))
    put_pieces(pick, 1, dot(chosen, out[...]).astype(BF16))


def weight_kernel(x, avg, dz, after, o):
    half = o.shape[0] // 2
    put_pieces(o.at[:half], 0, dot(x[...], dz[...], TN).astype(BF16))
    put_pieces(o.at[half:], 0, dot(avg[...], dz[...], TN).astype(BF16))


def back_kernel(dz, w, davg, am, ar, o, r):
    m = ar.shape[1]
    r[...] = dot(ar[m:, :], davg[...], TN)
    o[...] = dot(dz[...], w[...], NT) + dot(am[m:, :], davg[...], TN)
    o.send()


def mirror_back_kernel(back, a, got, o):
    put_pieces(o, 0, (back[...] + dot(a[...], get_pieces(got, 0), TN)).astype(BF16))


def master_back_kernel(back, a, got, o, out):
    o[...] = back[...] + dot(a[...], get_pieces(got, 0), TN)
    o.send()
    out[...] = get_pieces(got, 1)
    out.send()


def pack_kernel(rows, got, o):
    o[:, :TILE, :] = rows[...]
    total = jnp.sum(got[...].astype(F32), axis=0).astype(BF16)
    o[:, TILE:, :] = jnp.broadcast_to(total[None], (o.shape[0],) + total.shape)


def share_kernel(got, o):
    total = jnp.sum(got[:, TILE:, :].astype(F32), axis=0).astype(BF16)
    o[...] = jnp.broadcast_to(total[None], o.shape)


def grad_kernel(send, back, got, o):
    spread = scatter_matrix(index_row(send[...]), o.shape[0])
    o[...] = (back[...] + dot(spread, get_pieces(got, 0))).astype(BF16)
    o.send()


def widen_kernel(got, w_self, w_neigh):
    half = got.shape[0] // 2
    w_self[...] = get_pieces(got.at[:half], 0).astype(F32)
    w_self.send()
    w_neigh[...] = get_pieces(got.at[half:], 0).astype(F32)
    w_neigh.send()


def on_device(
    dom,
    grp,
    features,
    w_self,
    w_neigh,
    degree,
    send_rows,
    inner_tiles,
    inner_blocks,
    outer_tiles,
    outer_blocks,
    tile_counts,
    d_out,
    d_mirror,
):
    rows, width = features.shape
    peers, each = send_rows.shape
    mirrors = peers * each
    slots = rows + mirrors
    mm = 2 * width
    groups = lax.axis_size(grp)
    def exchange(values, axis):
        return lax.all_to_all(values, axis, split_axis=0, concat_axis=0, tiled=True)

    def parcel(count, many=peers):
        return sds((many, count * TILE, width), BF16)

    def wide(count, dtype=F32):
        return sds((count, width), dtype)

    send = send_rows.T
    degree_col = degree[:, None]

    got_h = exchange(
        call(first_kernel, parcel(2), (send, features, d_mirror), "vffv", mm * mirrors * rows, "pick_h"), dom
    )
    a_master, a_mirror, part_master, part_mirror, a_corner = call(
        adjacency_kernel,
        (sds((slots, rows), BF16), sds((slots, mirrors), BF16), wide(rows), wide(mirrors), sds((mirrors, mirrors), BF16)),
        (tile_counts, inner_blocks.T, outer_blocks.T, inner_tiles, outer_tiles, features),
        "sss" + "fff" + "fffvv",
        mm * slots * rows,
        "adjacency",
        40000000,
    )
    mirror_part = call(
        mirror_part_kernel, parcel(1), (part_mirror, a_corner, got_h), "vvvv", mm * mirrors * mirrors, "mirror_part", LITTLE
    )
    got_part = exchange(mirror_part, dom)
    p_master, z_self, g_out = call(
        master_part_kernel,
        (wide(rows),) * 3,
        (part_master, a_mirror, got_h, features, w_self, send, d_out),
        "ffvfvvf" + "fff",
        mm * rows * (2 * mirrors + width),
        "master_part",
    )
    avg, out, dz, d_avg, pick_g = call(
        dense_kernel,
        (wide(rows, BF16),) * 4 + (parcel(2),),
        (send, degree_col, p_master, z_self, g_out, got_part, w_neigh),
        "vffffvv" + "ffffv",
        mm * rows * (2 * mirrors + 2 * width),
        "dense",
    )
    got_g = exchange(pick_g, dom)
    back, back_mirror = call(
        back_kernel,
        (wide(rows), wide(mirrors)),
        (dz, w_self, d_avg, a_master, a_mirror),
        "fvfff" + "fv",
        mm * rows * (width + slots),
        "back",
    )
    terms = call(
        weight_kernel, parcel(1, groups), (features, avg, dz, back_mirror), "fff" + "x" + "v", 2 * mm * rows * width, "weights"
    )
    got_terms = exchange(terms, grp)
    mirror_back = call(
        mirror_back_kernel,
        parcel(1),
        (back_mirror, a_corner, got_g),
        "vvvv",
        mm * mirrors * mirrors,
        "mirror_back",
        LITTLE,
    )
    packed = call(pack_kernel, parcel(2), (mirror_back, got_terms), "vvv", 0, "pack", LITTLE)
    got_back = exchange(packed, dom)
    back, mirror_out = call(
        master_back_kernel,
        (wide(rows), wide(mirrors, BF16)),
        (back, a_master, got_g),
        ("f", mirrors, "v", "f", "f"),
        mm * rows * mirrors,
        "master_back",
    )
    shared = call(share_kernel, parcel(1, groups), (got_back,), "vv", 0, "share", LITTLE)
    totals = exchange(shared, grp)
    grad_h = call(
        grad_kernel, wide(rows, BF16), (send, back, got_back), "vfv" + "f", mm * rows * mirrors, "grad"
    )
    grad_wself, grad_wneigh = call(
        widen_kernel, (wide(width),) * 2, (totals,), "vff", 0, "widen", LITTLE
    )
    return (out, mirror_out, grad_h, grad_wself, grad_wneigh)


def solution(mesh):
    names = ("dom", "grp")
    split = lambda rank: P(names, *([None] * (rank - 1)))
    in_specs = (
        split(2), P(), P(), split(1), split(2), split(3), split(2), split(3), split(2), split(2),
        split(2), split(2),
    )
    out_specs = (split(2), split(2), split(2), P(), P())
    return jax.shard_map(
        functools.partial(on_device, "dom", "grp"),
        mesh=mesh, in_specs=in_specs, out_specs=out_specs, check_vma=False,
    )
```

```python
import functools

import jax
import jax.numpy as jnp
from jax import lax
from jax.experimental import pallas as pl
from jax.experimental.pallas import tpu as pltpu
from jax.sharding import PartitionSpec as P

BLOCK = 128
TILE = 16
BF16 = jnp.bfloat16
F32 = jnp.float32
NN = (((1,), (0,)), ((), ()))
TN = (((0,), (0,)), ((), ()))
NT = (((1,), (1,)), ((), ()))
ROOM = 62_500_000
LITTLE = 8_000_000


def dot(a, b, dims=NN):
    return lax.dot_general(a, b, dims, preferred_element_type=F32)


def one_hot(mask):
    return jnp.where(mask, 1.0, 0.0).astype(BF16)


def iota(shape, dim):
    return lax.broadcasted_iota(jnp.int32, shape, dim)


def narrow(value):
    return value.astype(F32).astype(BF16)


def index_column(send):
    each, peers = send.shape
    total = each * peers
    pick = one_hot(iota((total, peers), 0) // each == iota((total, peers), 1))
    full = dot(pick, narrow(send >> 5), NT) * 32.0 + dot(pick, narrow(send & 31), NT)
    mine = jnp.where(iota((total, each), 1) == iota((total, each), 0) % each, full, 0.0)
    return jnp.sum(mine, axis=1, keepdims=True).astype(jnp.int32)


def index_row(send):
    each, peers = send.shape
    total = each * peers
    pick = one_hot(iota((peers, total), 1) // each == iota((peers, total), 0))
    full = dot(narrow(send >> 5), pick) * 32.0 + dot(narrow(send & 31), pick)
    mine = jnp.where(iota((each, total), 0) == iota((each, total), 1) % each, full, 0.0)
    return jnp.sum(mine, axis=0, keepdims=True).astype(jnp.int32)


def gather_matrix(column, rows):
    return one_hot(iota((column.shape[0], rows), 1) == column)


def scatter_matrix(row, rows, first=0):
    return one_hot(iota((rows, row.shape[1]), 0) + first == row)


def put_pieces(ref, number, rows):
    ref[:, number * TILE : (number + 1) * TILE, :] = rows.reshape(ref.shape[0], TILE, ref.shape[2])


def get_pieces(ref, number):
    return ref[:, number * TILE : (number + 1) * TILE, :].reshape(ref.shape[0] * TILE, ref.shape[2])


class Far:
    def __init__(self, source, here, sem):
        self.here = here
        self.copy = pltpu.make_async_copy(source, here, sem)
        self.shape = here.shape
        self.copy.start()
        self.waiting = True

    def __getitem__(self, at):
        if self.waiting:
            self.copy.wait()
            self.waiting = False
        return self.here[at]


class FarOut:
    def __init__(self, target, here, sem):
        self.here = here
        self.copy = pltpu.make_async_copy(here, target, sem)
        self.shape = here.shape

    def __setitem__(self, at, value):
        self.here[at] = value

    def __getitem__(self, at):
        return self.here[at]

    def send(self):
        self.copy.start()


def sds(shape, dtype):
    return jax.ShapeDtypeStruct(shape, dtype)


def call(body, out, args, where, flops=0, name=None, room=ROOM):
    many = isinstance(out, tuple)
    outs = out if many else (out,)
    every = list(args) + list(outs)
    spaces, staged, shapes = [], [], []
    for value, mark in zip(every, where, strict=True):
        if mark == "v":
            spaces.append(pl.BlockSpec(memory_space=pltpu.VMEM))
        elif mark == "x":
            spaces.append(pl.BlockSpec(memory_space=pl.ANY))
        elif mark == "s":
            spaces.append(pl.BlockSpec(memory_space=pltpu.SMEM))
        else:
            spaces.append(pl.BlockSpec(memory_space=pltpu.HBM))
            shape = value.shape if mark == "f" else (mark,) + value.shape[1:]
            shapes.append(pltpu.VMEM(shape, value.dtype))
        staged.append(mark not in ("v", "s", "x"))
    count = len(shapes)

    def kernel(*refs):
        given = list(refs[: len(every)])
        scratch = list(refs[len(every) : len(every) + count])
        sems = refs[-1] if count else None
        used = 0
        late = []
        for k, far in enumerate(staged):
            if not far:
                continue
            here = scratch[used]
            if k < len(args):
                source = given[k] if where[k] == "f" else given[k].at[pl.ds(0, where[k])]
                given[k] = Far(source, here, sems.at[used])
            else:
                given[k] = FarOut(given[k], here, sems.at[used])
                late.append(given[k])
            used += 1
        body(*given)
        for item in given[: len(args)]:
            if isinstance(item, Far) and item.waiting:
                item.copy.wait()
        for item in late:
            item.copy.wait()

    moved = sum(v.size * v.dtype.itemsize for v in every)
    return pl.pallas_call(
        kernel,
        out_shape=out,
        in_specs=spaces[: len(args)],
        out_specs=tuple(spaces[len(args) :]) if many else spaces[-1],
        scratch_shapes=shapes + ([pltpu.SemaphoreType.DMA((count,))] if count else []),
        compiler_params=pltpu.CompilerParams(vmem_limit_bytes=room),
        cost_estimate=pl.CostEstimate(flops=flops, bytes_accessed=moved, transcendentals=0),
        name=name,
    )(*args)


def first_kernel(send, x, d, o):
    chosen = gather_matrix(index_column(send[...]), x.shape[0])
    put_pieces(o, 1, d[...])
    put_pieces(o, 0, dot(chosen, x[...]).astype(BF16))


def adjacency_kernel(counts, ib, ob, it, ot, x, master, mirror, part_master, part_mirror, mirror_mirror):
    masters = x.shape[0] // BLOCK
    mirrors = mirror.shape[1] // BLOCK
    master.here[...] = jnp.zeros(master.shape, BF16)
    mirror.here[...] = jnp.zeros(mirror.shape, BF16)

    def place(tiles, table, count, into, first):
        def step(k, carry):
            @pl.when(k < count)
            def _():
                dst = table[0, k]
                dst = jnp.where(dst >= masters, dst - masters, dst + mirrors)
                src = table[1, k] - first
                rows = pl.ds(pl.multiple_of(dst * BLOCK, BLOCK), BLOCK)
                cols = pl.ds(pl.multiple_of(src * BLOCK, BLOCK), BLOCK)
                into[rows, cols] = tiles[k]

            return carry

        lax.fori_loop(0, tiles.shape[0], step, 0)

    it.copy.wait()
    it.waiting = False
    ot.copy.wait()
    ot.waiting = False
    place(it.here, ib, counts[0, 0], master.here, 0)
    place(ot.here, ob, counts[0, 1], mirror.here, masters)
    master.send()
    mirror.send()
    size = mirrors * BLOCK
    mirror_mirror[...] = mirror[:size, :]
    part_mirror[...] = dot(master[:size, :], x[...])
    part_master[...] = dot(master[size:, :], x[...])
    part_master.send()


def mirror_part_kernel(part, a, got, o):
    rows = part[...] + dot(a[...], get_pieces(got, 0))
    put_pieces(o, 0, rows.astype(BF16))


def master_part_kernel(part, a, got, x, w, send, d, p, z, g):
    m = a.shape[1]
    z[...] = dot(x[...], w[...])
    z.send()
    p[...] = part[...] + dot(a[m:, :], get_pieces(got, 0))
    p.send()
    spread = scatter_matrix(index_row(send[...]), x.shape[0])
    g[...] = d[...].astype(F32) + dot(spread, get_pieces(got, 1))
    g.send()


def dense_kernel(send, deg, p, z, g, got, w, avg, out, dz, davg, pick):
    rows = p.shape[0]
    spread = scatter_matrix(index_row(send[...]), rows)
    chosen = gather_matrix(index_column(send[...]), rows)
    collected = dot(spread, get_pieces(got, 0))
    share = 1.0 / deg[...]
    mean = ((p[...] + collected) * share).astype(BF16)
    avg[...] = mean
    avg.send()
    zz = z[...] + dot(mean, w[...])
    s = jax.nn.sigmoid(zz)
    u = zz * s
    scale = lax.rsqrt(jnp.mean(u * u, axis=1, keepdims=True) + 1e-05)
    n = u * scale
    out[...] = n.astype(BF16)
    out.send()
    put_pieces(pick, 1, dot(chosen, out[...]).astype(BF16))
    gg = g[...]
    du = scale * (gg - n * jnp.mean(gg * n, axis=1, keepdims=True))
    dz[...] = (du * (s + u * (1.0 - s))).astype(BF16)
    dz.send()
    davg[...] = (dot(dz[...], w[...], NT) * share).astype(BF16)
    davg.send()
    put_pieces(pick, 0, dot(chosen, davg[...]).astype(BF16))


def weight_kernel(x, avg, dz, after, o):
    half = o.shape[0] // 2
    put_pieces(o.at[:half], 0, dot(x[...], dz[...], TN).astype(BF16))
    put_pieces(o.at[half:], 0, dot(avg[...], dz[...], TN).astype(BF16))


def back_kernel(dz, w, davg, am, ar, o, r):
    m = ar.shape[1]
    r[...] = dot(ar[m:, :], davg[...], TN)
    o[...] = dot(dz[...], w[...], NT) + dot(am[m:, :], davg[...], TN)
    o.send()


def mirror_back_kernel(back, a, got, o):
    put_pieces(o, 0, (back[...] + dot(a[...], get_pieces(got, 0), TN)).astype(BF16))


def master_back_kernel(back, a, got, o, out):
    o[...] = back[...] + dot(a[...], get_pieces(got, 0), TN)
    o.send()
    out[...] = get_pieces(got, 1)
    out.send()


def pack_kernel(rows, got, o):
    o[:, :TILE, :] = rows[...]
    total = jnp.sum(got[...].astype(F32), axis=0).astype(BF16)
    o[:, TILE:, :] = jnp.broadcast_to(total[None], (o.shape[0],) + total.shape)


def share_kernel(got, o):
    total = jnp.sum(got[:, TILE:, :].astype(F32), axis=0).astype(BF16)
    o[...] = jnp.broadcast_to(total[None], o.shape)


def grad_kernel(send, back, got, o):
    spread = scatter_matrix(index_row(send[...]), o.shape[0])
    o[...] = (back[...] + dot(spread, get_pieces(got, 0))).astype(BF16)
    o.send()


def widen_kernel(got, w_self, w_neigh):
    half = got.shape[0] // 2
    w_self[...] = get_pieces(got.at[:half], 0).astype(F32)
    w_self.send()
    w_neigh[...] = get_pieces(got.at[half:], 0).astype(F32)
    w_neigh.send()


def on_device(
    dom,
    grp,
    features,
    w_self,
    w_neigh,
    degree,
    send_rows,
    inner_tiles,
    inner_blocks,
    outer_tiles,
    outer_blocks,
    tile_counts,
    d_out,
    d_mirror,
):
    rows, width = features.shape
    peers, each = send_rows.shape
    mirrors = peers * each
    slots = rows + mirrors
    mm = 2 * width
    groups = lax.axis_size(grp)
    def exchange(values, axis):
        return lax.all_to_all(values, axis, split_axis=0, concat_axis=0, tiled=True)

    def parcel(count, many=peers):
        return sds((many, count * TILE, width), BF16)

    def wide(count, dtype=F32):
        return sds((count, width), dtype)

    send = send_rows.T
    degree_col = degree[:, None]

    got_h = exchange(
        call(first_kernel, parcel(2), (send, features, d_mirror), "vffv", mm * mirrors * rows, "pick_h"), dom
    )
    a_master, a_mirror, part_master, part_mirror, a_corner = call(
        adjacency_kernel,
        (sds((slots, rows), BF16), sds((slots, mirrors), BF16), wide(rows), wide(mirrors), sds((mirrors, mirrors), BF16)),
        (tile_counts, inner_blocks.T, outer_blocks.T, inner_tiles, outer_tiles, features),
        "sss" + "fff" + "fffvv",
        mm * slots * rows,
        "adjacency",
        40000000,
    )
    mirror_part = call(
        mirror_part_kernel, parcel(1), (part_mirror, a_corner, got_h), "vvvv", mm * mirrors * mirrors, "mirror_part", LITTLE
    )
    got_part = exchange(mirror_part, dom)
    p_master, z_self, g_out = call(
        master_part_kernel,
        (wide(rows),) * 3,
        (part_master, a_mirror, got_h, features, w_self, send, d_out),
        "ffvfvvf" + "fff",
        mm * rows * (2 * mirrors + width),
        "master_part",
    )
    avg, out, dz, d_avg, pick_g = call(
        dense_kernel,
        (wide(rows, BF16),) * 4 + (parcel(2),),
        (send, degree_col, p_master, z_self, g_out, got_part, w_neigh),
        "vffffvv" + "ffffv",
        mm * rows * (2 * mirrors + 2 * width),
        "dense",
    )
    got_g = exchange(pick_g, dom)
    back, back_mirror = call(
        back_kernel,
        (wide(rows), wide(mirrors)),
        (dz, w_self, d_avg, a_master, a_mirror),
        "fvfff" + "fv",
        mm * rows * (width + slots),
        "back",
    )
    terms = call(
        weight_kernel, parcel(1, groups), (features, avg, dz, back_mirror), "fff" + "x" + "v", 2 * mm * rows * width, "weights"
    )
    got_terms = exchange(terms, grp)
    mirror_back = call(
        mirror_back_kernel,
        parcel(1),
        (back_mirror, a_corner, got_g),
        "vvvv",
        mm * mirrors * mirrors,
        "mirror_back",
        LITTLE,
    )
    packed = call(pack_kernel, parcel(2), (mirror_back, got_terms), "vvv", 0, "pack", LITTLE)
    got_back = exchange(packed, dom)
    back, mirror_out = call(
        master_back_kernel,
        (wide(rows), wide(mirrors, BF16)),
        (back, a_master, got_g),
        ("f", mirrors, "v", "f", "f"),
        mm * rows * mirrors,
        "master_back",
    )
    shared = call(share_kernel, parcel(1, groups), (got_back,), "vv", 0, "share", LITTLE)
    totals = exchange(shared, grp)
    grad_h = call(
        grad_kernel, wide(rows, BF16), (send, back, got_back), "vfv" + "f", mm * rows * mirrors, "grad"
    )
    grad_wself, grad_wneigh = call(
        widen_kernel, (wide(width),) * 2, (totals,), "vff", 0, "widen", LITTLE
    )
    return (out, mirror_out, grad_h, grad_wself, grad_wneigh)


def solution(mesh):
    names = ("dom", "grp")
    split = lambda rank: P(names, *([None] * (rank - 1)))
    in_specs = (
        split(2), P(), P(), split(1), split(2), split(3), split(2), split(3), split(2), split(2),
        split(2), split(2),
    )
    out_specs = (split(2), split(2), split(2), P(), P())
    return jax.shard_map(
        functools.partial(on_device, "dom", "grp"),
        mesh=mesh, in_specs=in_specs, out_specs=out_specs, check_vma=False,
    )
```

```python
import functools

import jax
import jax.numpy as jnp
from jax import lax
from jax.experimental import pallas as pl
from jax.experimental.pallas import tpu as pltpu
from jax.sharding import PartitionSpec as P

BLOCK = 128
TILE = 16
BF16 = jnp.bfloat16
F32 = jnp.float32
NN = (((1,), (0,)), ((), ()))
TN = (((0,), (0,)), ((), ()))
NT = (((1,), (1,)), ((), ()))
ROOM = 62_500_000
LITTLE = 8_000_000


def dot(a, b, dims=NN):
    return lax.dot_general(a, b, dims, preferred_element_type=F32)


def one_hot(mask):
    return jnp.where(mask, 1.0, 0.0).astype(BF16)


def iota(shape, dim):
    return lax.broadcasted_iota(jnp.int32, shape, dim)


def narrow(value):
    return value.astype(F32).astype(BF16)


def index_column(send):
    each, peers = send.shape
    total = each * peers
    pick = one_hot(iota((total, peers), 0) // each == iota((total, peers), 1))
    full = dot(pick, narrow(send >> 5), NT) * 32.0 + dot(pick, narrow(send & 31), NT)
    mine = jnp.where(iota((total, each), 1) == iota((total, each), 0) % each, full, 0.0)
    return jnp.sum(mine, axis=1, keepdims=True).astype(jnp.int32)


def index_row(send):
    each, peers = send.shape
    total = each * peers
    pick = one_hot(iota((peers, total), 1) // each == iota((peers, total), 0))
    full = dot(narrow(send >> 5), pick) * 32.0 + dot(narrow(send & 31), pick)
    mine = jnp.where(iota((each, total), 0) == iota((each, total), 1) % each, full, 0.0)
    return jnp.sum(mine, axis=0, keepdims=True).astype(jnp.int32)


def gather_matrix(column, rows):
    return one_hot(iota((column.shape[0], rows), 1) == column)


def scatter_matrix(row, rows, first=0):
    return one_hot(iota((rows, row.shape[1]), 0) + first == row)


def put_pieces(ref, number, rows):
    ref[:, number * TILE : (number + 1) * TILE, :] = rows.reshape(ref.shape[0], TILE, ref.shape[2])


def get_pieces(ref, number):
    return ref[:, number * TILE : (number + 1) * TILE, :].reshape(ref.shape[0] * TILE, ref.shape[2])


class Far:
    def __init__(self, source, here, sem):
        self.here = here
        self.copy = pltpu.make_async_copy(source, here, sem)
        self.shape = here.shape
        self.copy.start()
        self.waiting = True

    def __getitem__(self, at):
        if self.waiting:
            self.copy.wait()
            self.waiting = False
        return self.here[at]


class FarOut:
    def __init__(self, target, here, sem):
        self.here = here
        self.copy = pltpu.make_async_copy(here, target, sem)
        self.shape = here.shape

    def __setitem__(self, at, value):
        self.here[at] = value

    def __getitem__(self, at):
        return self.here[at]

    def send(self):
        self.copy.start()


def sds(shape, dtype):
    return jax.ShapeDtypeStruct(shape, dtype)


def call(body, out, args, where, flops=0, name=None, room=ROOM):
    many = isinstance(out, tuple)
    outs = out if many else (out,)
    every = list(args) + list(outs)
    spaces, staged, shapes = [], [], []
    for value, mark in zip(every, where, strict=True):
        if mark == "v":
            spaces.append(pl.BlockSpec(memory_space=pltpu.VMEM))
        elif mark == "x":
            spaces.append(pl.BlockSpec(memory_space=pl.ANY))
        elif mark == "s":
            spaces.append(pl.BlockSpec(memory_space=pltpu.SMEM))
        else:
            spaces.append(pl.BlockSpec(memory_space=pltpu.HBM))
            shape = value.shape if mark == "f" else (mark,) + value.shape[1:]
            shapes.append(pltpu.VMEM(shape, value.dtype))
        staged.append(mark not in ("v", "s", "x"))
    count = len(shapes)

    def kernel(*refs):
        given = list(refs[: len(every)])
        scratch = list(refs[len(every) : len(every) + count])
        sems = refs[-1] if count else None
        used = 0
        late = []
        for k, far in enumerate(staged):
            if not far:
                continue
            here = scratch[used]
            if k < len(args):
                source = given[k] if where[k] == "f" else given[k].at[pl.ds(0, where[k])]
                given[k] = Far(source, here, sems.at[used])
            else:
                given[k] = FarOut(given[k], here, sems.at[used])
                late.append(given[k])
            used += 1
        body(*given)
        for item in given[: len(args)]:
            if isinstance(item, Far) and item.waiting:
                item.copy.wait()
        for item in late:
            item.copy.wait()

    moved = sum(v.size * v.dtype.itemsize for v in every)
    return pl.pallas_call(
        kernel,
        out_shape=out,
        in_specs=spaces[: len(args)],
        out_specs=tuple(spaces[len(args) :]) if many else spaces[-1],
        scratch_shapes=shapes + ([pltpu.SemaphoreType.DMA((count,))] if count else []),
        compiler_params=pltpu.CompilerParams(vmem_limit_bytes=room),
        cost_estimate=pl.CostEstimate(flops=flops, bytes_accessed=moved, transcendentals=0),
        name=name,
    )(*args)


def first_kernel(send, x, d, o):
    chosen = gather_matrix(index_column(send[...]), x.shape[0])
    put_pieces(o, 1, d[...])
    put_pieces(o, 0, dot(chosen, x[...]).astype(BF16))


def adjacency_kernel(counts, ib, ob, it, ot, x, master, mirror, part_master, part_mirror, mirror_mirror):
    masters = x.shape[0] // BLOCK
    mirrors = mirror.shape[1] // BLOCK
    master.here[...] = jnp.zeros(master.shape, BF16)
    mirror.here[...] = jnp.zeros(mirror.shape, BF16)

    def place(tiles, table, count, into, first):
        def step(k, carry):
            @pl.when(k < count)
            def _():
                dst = table[0, k]
                dst = jnp.where(dst >= masters, dst - masters, dst + mirrors)
                src = table[1, k] - first
                rows = pl.ds(pl.multiple_of(dst * BLOCK, BLOCK), BLOCK)
                cols = pl.ds(pl.multiple_of(src * BLOCK, BLOCK), BLOCK)
                into[rows, cols] = tiles[k]

            return carry

        lax.fori_loop(0, tiles.shape[0], step, 0)

    it.copy.wait()
    it.waiting = False
    ot.copy.wait()
    ot.waiting = False
    place(it.here, ib, counts[0, 0], master.here, 0)
    place(ot.here, ob, counts[0, 1], mirror.here, masters)
    master.send()
    mirror.send()
    size = mirrors * BLOCK
    mirror_mirror[...] = mirror[:size, :]
    part_mirror[...] = dot(master[:size, :], x[...])
    part_master[...] = dot(master[size:, :], x[...])
    part_master.send()


def mirror_part_kernel(part, a, got, o):
    rows = part[...] + dot(a[...], get_pieces(got, 0))
    put_pieces(o, 0, rows.astype(BF16))


def master_part_kernel(part, a, got, x, w, send, d, p, z, g):
    m = a.shape[1]
    z[...] = dot(x[...], w[...])
    z.send()
    p[...] = part[...] + dot(a[m:, :], get_pieces(got, 0))
    p.send()
    spread = scatter_matrix(index_row(send[...]), x.shape[0])
    g[...] = d[...].astype(F32) + dot(spread, get_pieces(got, 1))
    g.send()


def dense_kernel(send, deg, p, z, g, got, w, avg, out, dz, davg, pick):
    rows = p.shape[0]
    spread = scatter_matrix(index_row(send[...]), rows)
    chosen = gather_matrix(index_column(send[...]), rows)
    collected = dot(spread, get_pieces(got, 0))
    share = 1.0 / deg[...]
    mean = ((p[...] + collected) * share).astype(BF16)
    avg[...] = mean
    avg.send()
    zz = z[...] + dot(mean, w[...])
    s = jax.nn.sigmoid(zz)
    u = zz * s
    scale = lax.rsqrt(jnp.mean(u * u, axis=1, keepdims=True) + 1e-05)
    n = u * scale
    out[...] = n.astype(BF16)
    out.send()
    gg = g[...]
    du = scale * (gg - n * jnp.mean(gg * n, axis=1, keepdims=True))
    dz[...] = (du * (s + u * (1.0 - s))).astype(BF16)
    dz.send()
    davg[...] = (dot(dz[...], w[...], NT) * share).astype(BF16)
    davg.send()
    put_pieces(pick, 0, dot(chosen, davg[...]).astype(BF16))
    put_pieces(pick, 1, dot(chosen, out[...]).astype(BF16))


def weight_kernel(x, avg, dz, after, o):
    half = o.shape[0] // 2
    put_pieces(o.at[:half], 0, dot(x[...], dz[...], TN).astype(BF16))
    put_pieces(o.at[half:], 0, dot(avg[...], dz[...], TN).astype(BF16))


def back_kernel(dz, w, davg, am, ar, o, r):
    m = ar.shape[1]
    r[...] = dot(ar[m:, :], davg[...], TN)
    o[...] = dot(dz[...], w[...], NT) + dot(am[m:, :], davg[...], TN)
    o.send()


def mirror_back_kernel(back, a, got, o):
    put_pieces(o, 0, (back[...] + dot(a[...], get_pieces(got, 0), TN)).astype(BF16))


def master_back_kernel(back, a, got, o, out):
    o[...] = back[...] + dot(a[...], get_pieces(got, 0), TN)
    o.send()
    out[...] = get_pieces(got, 1)
    out.send()


def pack_kernel(rows, got, o):
    half = o.shape[2]
    total = jnp.sum(got[...].astype(F32), axis=0).astype(BF16)
    for side in range(2):
        columns = slice(side * half, (side + 1) * half)
        o[:, side * TILE : (side + 1) * TILE, :] = rows[:, :, columns]
    for peer in range(o.shape[0]):
        side = peer % 2
        o[peer, 2 * TILE :, :] = total[:, side * half : (side + 1) * half]


def share_kernel(got, o):
    total = jnp.sum(got[:, 2 * TILE :, :].astype(F32), axis=0).astype(BF16)
    o[...] = jnp.broadcast_to(total[None], o.shape)


def grad_kernel(send, back, got, o):
    spread = scatter_matrix(index_row(send[...]), o.shape[0])
    sides = [got[:, k * TILE : (k + 1) * TILE, :].reshape(got.shape[0] * TILE, got.shape[2]) for k in range(2)]
    o[...] = (back[...] + dot(spread, jnp.concatenate(sides, axis=1))).astype(BF16)
    o.send()


def widen_kernel(core, mine, other, w_self, w_neigh):
    half = mine.shape[2]
    rows = mine.shape[0] * mine.shape[1]
    ours = mine[...].reshape(rows, half).astype(F32)
    theirs = other[...].reshape(rows, half).astype(F32)
    first = core[0, 0] == 0
    left = jnp.where(first, ours, theirs)
    right = jnp.where(first, theirs, ours)
    for into, at in ((w_self, slice(0, rows // 2)), (w_neigh, slice(rows // 2, rows))):
        into[:, :half] = left[at, :]
        into[:, half:] = right[at, :]
        into.send()


def on_device(
    dom,
    grp,
    features,
    w_self,
    w_neigh,
    degree,
    send_rows,
    inner_tiles,
    inner_blocks,
    outer_tiles,
    outer_blocks,
    tile_counts,
    d_out,
    d_mirror,
):
    rows, width = features.shape
    peers, each = send_rows.shape
    mirrors = peers * each
    slots = rows + mirrors
    mm = 2 * width
    groups = lax.axis_size(grp)
    def exchange(values, axis):
        return lax.all_to_all(values, axis, split_axis=0, concat_axis=0, tiled=True)

    def parcel(count, many=peers):
        return sds((many, count * TILE, width), BF16)

    def wide(count, dtype=F32):
        return sds((count, width), dtype)

    send = send_rows.T
    degree_col = degree[:, None]

    got_h = exchange(
        call(first_kernel, parcel(2), (send, features, d_mirror), "vffv", mm * mirrors * rows, "pick_h"), dom
    )
    a_master, a_mirror, part_master, part_mirror, a_corner = call(
        adjacency_kernel,
        (sds((slots, rows), BF16), sds((slots, mirrors), BF16), wide(rows), wide(mirrors), sds((mirrors, mirrors), BF16)),
        (tile_counts, inner_blocks.T, outer_blocks.T, inner_tiles, outer_tiles, features),
        "sss" + "fff" + "fffvv",
        mm * slots * rows,
        "adjacency",
        40000000,
    )
    mirror_part = call(
        mirror_part_kernel, parcel(1), (part_mirror, a_corner, got_h), "vvvv", mm * mirrors * mirrors, "mirror_part", LITTLE
    )
    got_part = exchange(mirror_part, dom)
    p_master, z_self, g_out = call(
        master_part_kernel,
        (wide(rows),) * 3,
        (part_master, a_mirror, got_h, features, w_self, send, d_out),
        "ffvfvvf" + "fff",
        mm * rows * (2 * mirrors + width),
        "master_part",
    )
    avg, out, dz, d_avg, pick_g = call(
        dense_kernel,
        (wide(rows, BF16),) * 4 + (parcel(2),),
        (send, degree_col, p_master, z_self, g_out, got_part, w_neigh),
        "vffffvv" + "ffffv",
        mm * rows * (2 * mirrors + 2 * width),
        "dense",
    )
    got_g = exchange(pick_g, dom)
    back, back_mirror = call(
        back_kernel,
        (wide(rows), wide(mirrors)),
        (dz, w_self, d_avg, a_master, a_mirror),
        "fvfff" + "fv",
        mm * rows * (width + slots),
        "back",
    )
    terms = call(
        weight_kernel, parcel(1, groups), (features, avg, dz, back_mirror), "fff" + "x" + "v", 2 * mm * rows * width, "weights"
    )
    got_terms = exchange(terms, grp)
    mirror_back = call(
        mirror_back_kernel,
        parcel(1),
        (back_mirror, a_corner, got_g),
        "vvvv",
        mm * mirrors * mirrors,
        "mirror_back",
        LITTLE,
    )
    half = width // 2
    packed = call(
        pack_kernel, sds((peers, 3 * TILE, half), BF16), (mirror_back, got_terms), "vvv", 0, "pack", LITTLE
    )
    got_back = exchange(packed, dom)
    back, mirror_out = call(
        master_back_kernel,
        (wide(rows), wide(mirrors, BF16)),
        (back, a_master, got_g),
        ("f", mirrors, "v", "f", "f"),
        mm * rows * mirrors,
        "master_back",
    )
    shared = call(share_kernel, sds((groups, TILE, half), BF16), (got_back,), "vv", 0, "share", LITTLE)
    totals = exchange(shared, grp)
    grad_h = call(
        grad_kernel, wide(rows, BF16), (send, back, got_back), "vfv" + "f", mm * rows * mirrors, "grad"
    )
    other = lax.ppermute(totals, dom, [(k, k ^ 1) for k in range(peers)])
    core = (lax.axis_index(dom) % 2).astype(jnp.int32).reshape(1, 1)
    grad_wself, grad_wneigh = call(
        widen_kernel, (wide(width),) * 2, (core, totals, other), "svvff", 0, "widen", LITTLE
    )
    return (out, mirror_out, grad_h, grad_wself, grad_wneigh)


def solution(mesh):
    names = ("dom", "grp")
    split = lambda rank: P(names, *([None] * (rank - 1)))
    in_specs = (
        split(2), P(), P(), split(1), split(2), split(3), split(2), split(3), split(2), split(2),
        split(2), split(2),
    )
    out_specs = (split(2), split(2), split(2), P(), P())
    return jax.shard_map(
        functools.partial(on_device, "dom", "grp"),
        mesh=mesh, in_specs=in_specs, out_specs=out_specs, check_vma=False,
    )
```
